256 devices in a mesh: lat: 4 (over x_lo, core), lon: 64 (over x_hi, z, y).
Axes of the slice: x: 4 (x_hi: 2, x_lo: 2; x = x_hi * 2 + x_lo), y: 4, z: 8, core: 2. Of those that a mesh axis runs over, the one named last changes fastest.
Arguments:
- block_input: bfloat16 [4, 24, 1536, 192], P(None, 'lat', 'lon'), may hold values from -100 to 100
- cotangent: bfloat16 [4, 24, 1536, 192], P(None, 'lat', 'lon'), may hold values from -6 to 6
- first_gain: float32 [192], replicated, may hold values from 0.5 to 1.5
- second_gain: float32 [192], replicated, may hold values from 0.5 to 1.5
- input_weight: bfloat16 [192, 576], replicated, may hold values from -0.4375 to 0.4375
- output_weight: bfloat16 [192, 192], replicated, may hold values from -0.4375 to 0.4375
- up_weight: bfloat16 [192, 768], replicated, may hold values from -0.4375 to 0.4375
- down_weight: bfloat16 [768, 192], replicated, may hold values from -0.21875 to 0.21875
- bias_table: float32 [2, 4, 6, 23, 144], P(None, 'lat'), may hold values from -4.5 to 300
Outputs:
- grad_input: bfloat16 [4, 24, 1536, 192], P(None, 'lat', 'lon')
- bias_grad: float32 [2, 4, 6, 23, 144], P(None, 'lat')
The draws below stay inside these ranges and needn't reach their ends.
All inputs are finite; a program needn't handle non-finite values.
Results may differ from the reference program's by a relative error of at most 0.018.
Values may be sent and summed in bfloat16 or wider, within the bound.
A program may use at most 128 MiB of HBM per device.

```python
import math
import jax
import jax.numpy as jnp
from jax import lax

C = 192
HEADS = 6
FF = 768
WZ = 2
WH = 6
WW = 12
Z = 4
H = 24
W = 1536
ZT = 2
HT = 4


def draw_block_input(key, part):
    key = jax.random.fold_in(key, 11)
    key_base, key_rows, key_columns = jax.random.split(key, 3)
    base = jax.random.truncated_normal(key_base, -4.0, 4.0, (Z, H, W, C), jnp.float32)
    low_scale, high_scale = (math.log(0.5), math.log(5.0))
    row_scale = jnp.exp(jax.random.uniform(key_rows, (Z, H, W, 1), jnp.float32, low_scale, high_scale))
    column_scale = jnp.exp(jax.random.uniform(key_columns, (C,), jnp.float32, math.log(0.5), math.log(5.0)))
    return (base * row_scale * column_scale).astype(jnp.bfloat16)


def draw_bias_table(key, part):
    key = jax.random.fold_in(key, 23)
    key_base = jax.random.fold_in(key, 0)
    shape = (ZT, HT, HEADS, 2 * WW - 1, WZ * WZ * WH * WH)
    return jax.random.truncated_normal(key_base, -3.0, 3.0, shape, jnp.float32)


def level_of(stream_key, shape, cuts, low, top_value):
    def one(dim, blocks):
        steps = jax.random.uniform(jax.random.fold_in(jax.random.fold_in(stream_key, 6), dim), (blocks,), jnp.float32, low / len(cuts), top_value / len(cuts))
        return jnp.repeat(jnp.exp(steps), shape[dim] // blocks).reshape((-1,) + (1,) * (len(shape) - dim - 1))

    level = one(*cuts[0])
    for cut in cuts[1:]:
        level = level * one(*cut)
    return level


def normal_values(rng, shape, scale, reach, pieces=(), held_as=jnp.bfloat16):
    loudness = level_of(rng, shape, pieces, -0.22, 0.18) if pieces else 1.0
    array = jax.random.normal(rng, shape, jnp.float32) * scale * loudness
    return jnp.minimum(jnp.maximum(array, -reach), reach).astype(held_as)


def setup_inputs(seed: int = 0) -> dict:
    seeds = jax.random.split(jax.random.key(seed), 10)
    block_input = draw_block_input(jax.random.fold_in(seeds[9], 71), 0)
    cotangent = normal_values(seeds[1], (Z, H, W, C), 1.0, 6.0, ((1, 4), (2, 64)))
    first_gain = jnp.clip(jax.random.uniform(seeds[2], (C,), jnp.float32, 0.5, 1.5), 0.5, 1.5)
    second_gain = jnp.clip(jax.random.uniform(seeds[3], (C,), jnp.float32, 0.5, 1.5), 0.5, 1.5)
    input_weight = normal_values(seeds[4], (C, 3 * C), C ** -0.5, 0.4375)
    output_weight = normal_values(seeds[5], (C, C), C ** -0.5, 0.4375)
    up_weight = normal_values(seeds[6], (C, FF), C ** -0.5, 0.4375)
    down_weight = normal_values(seeds[7], (FF, C), FF ** -0.5, 0.21875)
    bias_table = draw_bias_table(jax.random.fold_in(seeds[9], 71), 0)
    return dict(block_input=block_input, cotangent=cotangent, first_gain=first_gain, second_gain=second_gain, input_weight=input_weight, output_weight=output_weight, up_weight=up_weight, down_weight=down_weight, bias_table=bias_table)


EPSILON = 1e-05
EXCLUDED = -1000000000.0

def norm_rows(values, gain):
    average = lax.optimization_barrier(jnp.mean(values, axis=-1, keepdims=True))
    centred = values - average
    spread = lax.optimization_barrier(jnp.mean(centred * centred, axis=-1, keepdims=True))
    return centred * lax.rsqrt(spread + EPSILON) * gain

def first_norm(values, gain):
    return norm_rows(values, gain).astype(jnp.bfloat16)

def block_tail(values, attention, gain, up_weight, down_weight):
    channel_count = values.shape[-1]
    residual = values + attention.astype(jnp.float32)
    normed = norm_rows(residual, gain).astype(jnp.bfloat16)
    hidden = jnp.dot(normed.reshape(-1, channel_count), up_weight, preferred_element_type=jnp.float32)
    active = jax.nn.gelu(hidden, approximate=False).astype(jnp.bfloat16)
    mixed = jnp.dot(active, down_weight, preferred_element_type=jnp.float32)
    return residual + mixed.reshape(residual.shape)

def expand_bias(bias_table):
    zone_count, band_count, head_count = (bias_table.shape[0], bias_table.shape[1], bias_table.shape[2])
    offsets = jnp.arange(WW, dtype=jnp.int32)
    relative = offsets[:, None] - offsets[None, :] + WW - 1
    selector = (relative[:, :, None] == jnp.arange(2 * WW - 1, dtype=jnp.int32)[None, None, :]).astype(jnp.float32)
    table_parts = bias_table.reshape(zone_count, band_count, head_count, 2 * WW - 1, WZ, WZ, WH, WH)
    expanded = jnp.einsum('abnrpqst,ejr->abnpseqtj', table_parts, selector, precision=lax.Precision.HIGHEST)
    return expanded.reshape(zone_count, band_count, head_count, WZ * WH * WW, WZ * WH * WW)

def region_labels(zone_count, band_count, row_start, height, level_count):
    level_index = jnp.arange(zone_count * WZ, dtype=jnp.int32).reshape(zone_count, 1, WZ, 1, 1)
    row_index = row_start + jnp.arange(band_count * WH, dtype=jnp.int32).reshape(1, band_count, 1, WH, 1)
    level_mark = (level_index >= level_count - WZ // 2).astype(jnp.int32)
    row_mark = (row_index >= height - WH // 2).astype(jnp.int32)
    labels = jnp.broadcast_to(2 * level_mark + row_mark, (zone_count, band_count, WZ, WH, WW))
    return labels.reshape(zone_count, band_count, WZ * WH * WW)

def attend(block, bias_table, input_weight, output_weight, row_start, height):
    level_count, row_count, column_count, channel_count = block.shape
    zone_count = level_count // WZ
    band_count = row_count // WH
    sector_count = column_count // WW
    window_size = WZ * WH * WW
    head_size = channel_count // HEADS
    windows = block.reshape(zone_count, WZ, band_count, WH, sector_count, WW, channel_count)
    windows = windows.transpose(0, 2, 4, 1, 3, 5, 6).reshape(-1, channel_count)
    projected = jnp.dot(windows, input_weight, preferred_element_type=jnp.float32).astype(jnp.bfloat16)
    projected = projected.reshape(zone_count, band_count, sector_count, window_size, 3, HEADS, head_size)
    queries = projected[:, :, :, :, 0].astype(jnp.float32)
    key_part = projected[:, :, :, :, 1].astype(jnp.float32)
    value_part = projected[:, :, :, :, 2].astype(jnp.float32)
    scores = jnp.einsum('abwqnd,abwknd->abwnqk', queries, key_part) * head_size ** (-0.5)
    scores = scores + expand_bias(bias_table)[:, :, None]
    labels = region_labels(zone_count, band_count, row_start, height, level_count)
    allowed = labels[:, :, :, None] == labels[:, :, None, :]
    scores = jnp.where(allowed[:, :, None, None], scores, EXCLUDED)
    largest = lax.optimization_barrier(jnp.max(scores, axis=-1, keepdims=True))
    weights = jnp.exp(scores - largest)
    probs = (weights / lax.optimization_barrier(jnp.sum(weights, axis=-1, keepdims=True))).astype(jnp.bfloat16)
    mixed = jnp.einsum('abwnqk,abwknd->abwqnd', probs.astype(jnp.float32), value_part).astype(jnp.bfloat16)
    output = jnp.dot(mixed.reshape(-1, channel_count), output_weight, preferred_element_type=jnp.float32).astype(jnp.bfloat16)
    output = output.reshape(zone_count, band_count, sector_count, WZ, WH, WW, channel_count)
    return output.transpose(0, 3, 1, 4, 2, 5, 6).reshape(level_count, row_count, column_count, channel_count)

def reference(block_input, cotangent, first_gain, second_gain, input_weight, output_weight, up_weight, down_weight, bias_table):
    ahead = (-(WZ // 2), -(WH // 2), -(WW // 2))
    behind = (WZ // 2, WH // 2, WW // 2)
    inputs_wide = block_input.astype(jnp.float32)
    normed, norm_back = jax.vjp(lambda values: first_norm(values, first_gain), inputs_wide)
    rolled = jnp.roll(normed, ahead, (0, 1, 2))
    band_total = H // WH

    def band_forward(band):
        rows_block = lax.dynamic_slice_in_dim(rolled, band * WH, WH, 1)
        table_piece = lax.dynamic_slice_in_dim(bias_table, band, 1, 1)
        return attend(rows_block, table_piece, input_weight, output_weight, band * WH, H)
    stacked = lax.map(band_forward, jnp.arange(band_total, dtype=jnp.int32))
    attention_rolled = stacked.transpose(1, 0, 2, 3, 4).reshape(Z, H, W, C)
    attention = jnp.roll(attention_rolled, behind, (0, 1, 2))
    _, tail_back = jax.vjp(lambda values, extra: block_tail(values, extra, second_gain, up_weight, down_weight), inputs_wide, attention)
    grad_direct, grad_attention = tail_back(cotangent.astype(jnp.float32))
    grad_rolled = jnp.roll(grad_attention, ahead, (0, 1, 2))

    def band_backward(band):
        rows_block = lax.dynamic_slice_in_dim(rolled, band * WH, WH, 1)
        table_piece = lax.dynamic_slice_in_dim(bias_table, band, 1, 1)
        grad_rows = lax.dynamic_slice_in_dim(grad_rolled, band * WH, WH, 1)
        _, attend_back = jax.vjp(lambda rows_in, table_in: attend(rows_in, table_in, input_weight, output_weight, band * WH, H), rows_block, table_piece)
        return attend_back(grad_rows)
    grad_stacked, bias_parts = lax.map(band_backward, jnp.arange(band_total, dtype=jnp.int32))
    grad_window = grad_stacked.transpose(1, 0, 2, 3, 4).reshape(Z, H, W, C)
    bias_grad = bias_parts.transpose(1, 0, 2, 3, 4, 5).reshape(ZT, HT, HEADS, 2 * WW - 1, WZ * WZ * WH * WH)
    grad_norm = jnp.roll(grad_window, behind, (0, 1, 2))
    grad_front, = norm_back(grad_norm)
    grad_input = (grad_front + grad_direct).astype(jnp.bfloat16)
    return (grad_input, bias_grad)
```

```python
import functools
import numpy as np
import jax
import jax.numpy as jnp
from jax import lax
from jax.experimental import pallas as pl
from jax.experimental.pallas import tpu as pltpu

BF = jnp.bfloat16
F32 = jnp.float32
HEADS, WZ, WH, WW = 6, 2, 6, 12
HD = 32
C = 192
FF = 768
N = 144
PS = WZ * WH
OFFS = 2 * WW - 1
LW = 384
EPS = 1e-05
SCALE = HD ** -0.5
NEG = -1e30


def nn(a, b):
    return lax.dot_general(a, b, (((1,), (0,)), ((), ())), preferred_element_type=F32)


def nt(a, b):
    return lax.dot_general(a, b, (((1,), (1,)), ((), ())), preferred_element_type=F32)


def tn(a, b):
    return lax.dot_general(a, b, (((0,), (0,)), ((), ())), preferred_element_type=F32)


def spread_consts():
    spread = np.zeros((N, PS, LW), np.float32)
    for p in range(WZ):
        for q in range(WZ):
            for s in range(WH):
                for t in range(WH):
                    m = ((p * WZ + q) * WH + s) * WH + t
                    for r in range(OFFS):
                        spread[m, q * WH + t, r * PS + p * WH + s] = 1
    pick = np.zeros((24, LW), np.float32)
    for r in range(OFFS):
        pick[r, r * PS:(r + 1) * PS] = 1
    return spread.reshape(N, PS * LW), pick


def normalize(v):
    centred = v - jnp.mean(v, axis=-1, keepdims=True)
    rs = lax.rsqrt(jnp.mean(centred * centred, axis=-1, keepdims=True) + EPS)
    return centred * rs, rs


def norm_back(g, xh, rs):
    return rs * (g - jnp.mean(g, axis=-1, keepdims=True) - xh * jnp.mean(g * xh, axis=-1, keepdims=True))


def gelu_slope(h):
    cdf = 0.5 + 0.5 * lax.erf(h * 0.7071067811865476)
    return cdf + h * (jnp.exp(-0.5 * (h * h)) * 0.3989422804014327)


def expand_bias(lat, tb_ref, spread_ref, pick_ref, t24, strips, bias):
    t24[...] = jnp.zeros_like(t24)
    t24[:, 0:OFFS, :] = tb_ref[...]
    table = t24[...].reshape(12 * 24, N)
    hi = table.astype(BF)
    rest = table - hi.astype(F32)
    mid = rest.astype(BF)
    low = (rest - mid.astype(F32)).astype(BF)
    pick = pick_ref[...][None]
    for qt in range(PS):
        sel = spread_ref[:, qt * LW:(qt + 1) * LW]
        wide = nn(hi, sel) + nn(mid, sel) + nn(low, sel)
        strips[:, qt, :] = jnp.sum(wide.reshape(12, 24, LW) * pick, axis=1)
    row = lax.broadcasted_iota(jnp.int32, (N, N), 0).astype(F32)
    col = lax.broadcasted_iota(jnp.int32, (N, N), 1).astype(F32)

    def place(v):
        ps = v - PS * jnp.floor((v + 0.5) * (1.0 / PS))
        upper = (ps >= WH).astype(F32)
        s = ps - WH * upper
        return upper, (s >= WH // 2).astype(F32)

    rp, rs = place(row)
    cp, cs = place(col)
    last_band = (lat == 3).astype(F32)
    apart_rows = jnp.abs(rs - cs) * last_band
    apart_levels = jnp.abs(rp - cp)

    def one(an, carry):
        strip = strips[an]
        top = jnp.where(an >= HEADS, 1.0, 0.0)
        apart = (apart_rows + apart_levels * top) > 0.5
        for j in range(WW):
            part = strip[0:PS, (WW - 1 - j) * PS:(WW - 1 - j) * PS + N]
            bias[an, j * PS:(j + 1) * PS, :] = part
        bias[an] = jnp.where(apart, NEG, bias[an])
        return carry

    lax.fori_loop(0, 12, one, 0)


def window_step(w, a, c, x, ct, g1, g2, wi_ref, wit, wk, wv, wo_ref, wu_ref, wd_ref,
                bias, qbd, dobd, probs, mixed, qkvt, dqkvt, dbias):
    x = x.astype(F32)
    ct32 = ct.astype(F32)
    xh1, rs1 = normalize(x)
    xn1 = (xh1 * g1).astype(BF)
    qkvt[...] = nt(wit[...], xn1).astype(BF)
    keys = nn(xn1, wk[...]).astype(BF)
    values = nn(xn1, wv[...]).astype(BF)
    for n in range(HEADS):
        qbd[n * HD:(n + 1) * HD, n * 256:n * 256 + N] = qkvt[n * HD:(n + 1) * HD, :]
    for n in range(HEADS):
        s = nn(keys, qbd[:, n * 256:n * 256 + N]) * SCALE + bias[a * HEADS + n]
        e = jnp.exp(s - jnp.max(s, axis=0, keepdims=True))
        p = (e * (1.0 / jnp.sum(e, axis=0, keepdims=True))).astype(BF)
        probs[n] = p
        vt = qkvt[2 * C + n * HD:2 * C + (n + 1) * HD, :]
        mixed[n * HD:(n + 1) * HD, :] = nn(vt, p).astype(BF)
    attn = tn(mixed[...], wo_ref[...]).astype(BF)
    y = x + attn.astype(F32)
    xh2, rs2 = normalize(y)
    xn2 = (xh2 * g2).astype(BF)
    dxn2 = jnp.zeros((N, C), F32)
    for f in range(FF // 256):
        up = wu_ref[:, f * 256:(f + 1) * 256]
        h = nn(xn2, up)
        da = nt(ct, wd_ref[f * 256:(f + 1) * 256, :])
        dh = (da * gelu_slope(h)).astype(BF)
        dxn2 = dxn2 + nt(dh, up)
    dy = ct32 + norm_back(dxn2 * g2, xh2, rs2)
    gattn = dy.astype(BF)
    dot_ = nt(wo_ref[...], gattn).astype(BF)
    for n in range(HEADS):
        dobd[n * HD:(n + 1) * HD, n * 256:n * 256 + N] = dot_[n * HD:(n + 1) * HD, :]
    for n in range(HEADS):
        r = slice(n * HD, (n + 1) * HD)
        dp = nn(values, dobd[:, n * 256:n * 256 + N])
        p = probs[n].astype(F32)
        pd = p * dp
        ds = pd - p * jnp.sum(pd, axis=0, keepdims=True)
        if c == 0:
            dbias[a * HEADS + n] = ds
        else:
            dbias[a * HEADS + n] += ds
        dsb = ds.astype(BF)
        dqkvt[n * HD:(n + 1) * HD, :] = (nn(qkvt[C + n * HD:C + (n + 1) * HD, :], dsb) * SCALE).astype(BF)
        dqkvt[C + n * HD:C + (n + 1) * HD, :] = (nt(qkvt[n * HD:(n + 1) * HD, :], dsb) * SCALE).astype(BF)
        dqkvt[2 * C + n * HD:2 * C + (n + 1) * HD, :] = nt(dot_[r, :], probs[n]).astype(BF)
    dxn1 = nn(wi_ref[...], dqkvt[...]).astype(BF).T.astype(F32)
    return (dy + norm_back(dxn1 * g1, xh1, rs1)).astype(BF)


def fold_bias(dbias, spread_ref, pick_ref, strips, folded):
    strips[...] = jnp.zeros_like(strips)

    def one(an, carry):
        total = jnp.zeros((PS, LW), F32)
        for j in range(WW):
            part = dbias[an, j * PS:(j + 1) * PS, :]
            lo = (WW - 1 - j) * PS
            total = total + jnp.pad(part, ((0, 0), (lo, LW - N - lo)))
        strips[an, 0:PS, :] = total
        return carry

    lax.fori_loop(0, 12, one, 0)
    pick = pick_ref[...][None]
    total = jnp.zeros((12 * 24, N), F32)
    for qt in range(PS):
        rows = strips[:, qt, :][:, None, :] * pick
        total = total + nt(rows.reshape(12 * 24, LW).astype(BF), spread_ref[:, qt * LW:(qt + 1) * LW])
    folded[...] = total.reshape(12, 24, N)


def prepare_weights(wi_ref, wit, wk, wv):
    wit[...] = wi_ref[...].T
    wk[...] = wi_ref[:, C:2 * C]
    wv[...] = wi_ref[:, 2 * C:3 * C]


def main_kernel(xw, cw, g1_ref, g2_ref, wi_ref, wo_ref, wu_ref, wd_ref, tb_ref, spread_ref, pick_ref,
                gi, red, t24, strips, bias, wit, wk, wv, qbd, dobd, probs, mixed, qkvt, dqkvt, dbias, folded):
    lat = lax.axis_index("lat")
    prepare_weights(wi_ref, wit, wk, wv)
    expand_bias(lat, tb_ref, spread_ref, pick_ref, t24, strips, bias)
    qbd[...] = jnp.zeros_like(qbd)
    dobd[...] = jnp.zeros_like(dobd)
    g1, g2 = g1_ref[...], g2_ref[...]

    def zone(a, carry):
        for c in range(2):
            w = a * 2 + c
            rows = pl.ds(pl.multiple_of(w * N, N), N)
            gi[rows, :] = window_step(
                w, a, c, xw[rows, :], cw[rows, :], g1, g2, wi_ref, wit, wk, wv, wo_ref, wu_ref, wd_ref, bias,
                qbd.at[c], dobd.at[c], probs.at[c], mixed.at[c], qkvt.at[c], dqkvt.at[c], dbias)
        return carry

    lax.fori_loop(0, 2, zone, 0)
    fold_bias(dbias, spread_ref, pick_ref, strips, folded)
    pack_fold(folded, red)


def pack_fold(folded, red):
    for s in range(6):
        red[s] = folded[2 * s:2 * s + 2, :, 0:128].reshape(48, 128).astype(BF)
    red[7] = jnp.zeros((48, 128), BF)
    lane = lax.broadcasted_iota(jnp.int32, (24, 128), 1)
    for half in range(2):
        total = jnp.zeros((24, 128), F32)
        for k in range(8 if half == 0 else 4):
            tail = jnp.concatenate([folded[half * 8 + k][:, 128:N], jnp.zeros((24, 112), F32)], axis=1)
            total = total + (pltpu.roll(tail, 16 * k, 1) if k else tail)
        red[6, half * 24:(half + 1) * 24, :] = total.astype(BF)


VM = pl.BlockSpec(memory_space=pltpu.VMEM)

MAIN_SCRATCH = [
    pltpu.VMEM((12, 24, N), F32),
    pltpu.VMEM((12, 16, LW), F32),
    pltpu.VMEM((12, N, N), F32),
    pltpu.VMEM((3 * C, C), BF),
    pltpu.VMEM((C, C), BF),
    pltpu.VMEM((C, C), BF),
    pltpu.VMEM((2, C, HEADS * 256), BF),
    pltpu.VMEM((2, C, HEADS * 256), BF),
    pltpu.VMEM((2, HEADS, N, N), BF),
    pltpu.VMEM((2, C, N), BF),
    pltpu.VMEM((2, 3 * C, N), BF),
    pltpu.VMEM((2, 3 * C, N), BF),
    pltpu.VMEM((12, N, N), F32),
    pltpu.VMEM((12, 24, N), F32),
]


def main_call(xw, cw, g1, g2, wi, wo, wu, wd, tb, spread, pick):
    return pl.pallas_call(
        main_kernel,
        out_shape=(jax.ShapeDtypeStruct((4 * N, C), BF), jax.ShapeDtypeStruct((8, 48, 128), BF)),
        in_specs=[VM] * 11,
        out_specs=(VM, VM),
        scratch_shapes=MAIN_SCRATCH,
        compiler_params=pltpu.CompilerParams(vmem_limit_bytes=48 * 1024 * 1024),
    )(xw, cw, g1, g2, wi, wo, wu, wd, tb, spread, pick)


PIECE0, PIECE1 = 80, 48
LAT0, LAT1, OWN1, LON1, DIAG1, ROWS = 80, 160, 208, 256, 304, 352
MESH = pl.DeviceIdType.MESH


def piece_consts():
    pack = np.zeros((2, ROWS, N), np.float32)
    place0 = np.zeros((N, LAT1), np.float32)
    place1 = np.zeros((N, ROWS - LAT1), np.float32)
    for p in range(2):
        for h in range(6):
            own = h >= 3
            s = h - 3 if own else h + 3
            for w in range(24):
                e = (w - 6) % 24
                if e < 12:
                    row = (0 if own else LAT0) + (e * 2 + p) * 3 + s % 3
                    place0[e * PS + p * WH + s, row] = 1
                else:
                    e -= 12
                    base = (OWN1 if own else LAT1) if e < 6 else (LON1 if own else DIAG1)
                    row = base + ((e % 6) * 2 + p) * 3 + s % 3
                    place1[e * PS + p * WH + s, row - LAT1] = 1
                pack[p, row, h * 24 + w] = 1
    return pack, place0, place1


def lat_lon():
    return lax.axis_index("lat"), lax.axis_index("lon")


def shifted(lat, lon, da, do):
    return lax.rem(lat + 4 + da, 4), lax.rem(lon + 64 + do, 64)


def in_kernel(x_ref, ct_ref, pack_ref, place0_ref, place1_ref, xw, cw, out_box, land, send_sem, recv_sem):
    lat, lon = lat_lon()
    barrier = pltpu.get_barrier_semaphore()
    for da, do in ((1, 0), (0, 1), (1, 1)):
        pl.semaphore_signal(barrier, inc=1, device_id=shifted(lat, lon, da, do), device_id_type=MESH)
    for a in range(2):
        for k, ref in enumerate((x_ref, ct_ref)):
            piece = (nn(pack_ref[0], ref[(2 * a + 1) % 4]) + nn(pack_ref[1], ref[(2 * a + 2) % 4])).astype(BF)
            lanes = slice(k * C, (k + 1) * C)
            land[a, 0:LAT0, lanes] = piece[0:LAT0]
            land[a, OWN1:LON1, lanes] = piece[OWN1:LON1]
            out_box[a, 0:128, lanes] = piece[LAT0:OWN1]
            out_box[a, 128:224, lanes] = piece[LON1:ROWS]
        if a == 0:
            pl.semaphore_wait(barrier, 3)
        for copy in in_copies(a, lat, lon, out_box, land, send_sem, recv_sem):
            copy.start()
    for a in range(2):
        for copy in in_copies(a, lat, lon, out_box, land, send_sem, recv_sem):
            copy.wait()
        first = nn(place0_ref[...], land[a, 0:LAT1, :]).astype(BF)
        second = nn(place1_ref[...], land[a, LAT1:ROWS, :]).astype(BF)
        for k, ref in enumerate((xw, cw)):
            ref[2 * a * N:(2 * a + 1) * N, :] = first[:, k * C:(k + 1) * C]
            ref[(2 * a + 1) * N:(2 * a + 2) * N, :] = second[:, k * C:(k + 1) * C]


def in_copies(a, lat, lon, out_box, land, send_sem, recv_sem):
    plan = ((0, 128, LAT0, (-1, 0)), (128, 48, LON1, (0, -1)), (176, 48, DIAG1, (-1, -1)))
    return [
        pltpu.make_async_remote_copy(
            src_ref=out_box.at[a, pl.ds(start, size)],
            dst_ref=land.at[a, pl.ds(target, size)],
            send_sem=send_sem.at[a, k],
            recv_sem=recv_sem.at[a, k],
            device_id=shifted(lat, lon, *step),
            device_id_type=MESH,
        )
        for k, (start, size, target, step) in enumerate(plan)
    ]


def back_copies(a, lat, lon, box, land, send_sem, recv_sem):
    plan = ((LAT0, 128, (1, 0)), (LON1, 48, (0, 1)), (DIAG1, 48, (1, 1)))
    return [
        pltpu.make_async_remote_copy(
            src_ref=box.at[a, pl.ds(start, size)],
            dst_ref=land.at[a, pl.ds(start, size)],
            send_sem=send_sem.at[a, k],
            recv_sem=recv_sem.at[a, k],
            device_id=shifted(lat, lon, *step),
            device_id_type=MESH,
        )
        for k, (start, size, step) in enumerate(plan)
    ]


def deep_peer(lon, d):
    high, z, y = lon // 32, lax.rem(lon // 4, 8), lax.rem(lon, 4)
    return (high * 8 + lax.rem(z + d, 8)) * 4 + y


def flat_peer(lon, d):
    z = lax.rem(lon // 4, 8)
    place = lax.rem((lon // 32) * 4 + lax.rem(lon, 4) + d, 8)
    return ((place // 4) * 8 + z) * 4 + lax.rem(place, 4)


def sum_copies(kind, lat, lon, src, dst, send_sem, recv_sem):
    z = lax.rem(lon // 4, 8)
    copies = []
    for d in range(1, 8):
        if kind == 0:
            peer = deep_peer(lon, d)
            source, target = src.at[lax.rem(z + d, 8)], dst.at[d - 1]
        elif kind == 1:
            peer = flat_peer(lon, d)
            source, target = src, dst.at[d - 1]
        else:
            peer = deep_peer(lon, d)
            source, target = src, dst.at[z]
        copies.append(pltpu.make_async_remote_copy(
            src_ref=source, dst_ref=target, send_sem=send_sem.at[kind, d - 1], recv_sem=recv_sem.at[kind, d - 1],
            device_id=(lat, peer), device_id_type=MESH))
    return copies


def add_up(own, slots):
    total = own.astype(F32)
    for d in range(7):
        total = total + slots[d].astype(F32)
    return total.astype(BF)


def out_kernel(gi_ref, red_ref, unpack_ref, unplace0_ref, unplace1_ref, gx_ref, gb_ref,
               box, land, slots1, part, slots2, whole, full, send_sem, recv_sem, sum_send, sum_recv):
    lat, lon = lat_lon()
    z = lax.rem(lon // 4, 8)
    barrier = pltpu.get_barrier_semaphore()
    for da, do in ((-1, 0), (0, -1), (-1, -1)):
        pl.semaphore_signal(barrier, inc=1, device_id=shifted(lat, lon, da, do), device_id_type=MESH)
    for d in range(1, 8):
        pl.semaphore_signal(barrier, inc=1, device_id=(lat, deep_peer(lon, d)), device_id_type=MESH)
        pl.semaphore_signal(barrier, inc=1, device_id=(lat, flat_peer(lon, d)), device_id_type=MESH)
    pl.semaphore_wait(barrier, 17)
    phase1 = sum_copies(0, lat, lon, red_ref, slots1, sum_send, sum_recv)
    for copy in phase1:
        copy.start()
    halos = [back_copies(a, lat, lon, box, land, send_sem, recv_sem) for a in range(2)]
    for a in range(2):
        first = nn(unplace0_ref[...], gi_ref[2 * a * N:(2 * a + 1) * N, :]).astype(BF)
        second = nn(unplace1_ref[...], gi_ref[(2 * a + 1) * N:(2 * a + 2) * N, :]).astype(BF)
        land[a, 0:LAT0, :] = first[0:LAT0]
        land[a, OWN1:LON1, :] = second[OWN1 - LAT1:LON1 - LAT1]
        box[a, LAT0:LAT1, :] = first[LAT0:LAT1]
        box[a, LAT1:OWN1, :] = second[0:OWN1 - LAT1]
        box[a, LON1:ROWS, :] = second[LON1 - LAT1:]
        for copy in halos[a]:
            copy.start()
    for copy in phase1:
        copy.wait()
    part[...] = add_up(red_ref[z], slots1)
    phase2 = sum_copies(1, lat, lon, part, slots2, sum_send, sum_recv)
    for copy in phase2:
        copy.start()
    for a in range(2):
        for copy in halos[a]:
            copy.wait()
        for p in range(2):
            gx_ref[(2 * a + 1 + p) % 4] = nn(unpack_ref[p], land[a]).astype(BF)
    for copy in phase2:
        copy.wait()
    whole[...] = add_up(part[...], slots2)
    phase3 = sum_copies(2, lat, lon, whole, full, sum_send, sum_recv)
    for copy in phase3:
        copy.start()
    full[z] = whole[...]
    for copy in phase3:
        copy.wait()
    for s in range(6):
        gb_ref[2 * s:2 * s + 2, :, 0:128] = full[s].astype(F32).reshape(2, 24, 128)[:, 0:OFFS]
    for half in range(2):
        tails = full[6, half * 24:(half + 1) * 24, :].astype(F32)
        for k in range(8 if half == 0 else 4):
            gb_ref[half * 8 + k, :, 128:N] = tails[0:OFFS, 16 * k:16 * (k + 1)]


def in_call(x, ct, pack, place0, place1):
    box = jax.ShapeDtypeStruct((4 * N, C), BF)
    return pl.pallas_call(
        in_kernel,
        out_shape=(box, box),
        in_specs=[VM] * 5,
        out_specs=(VM, VM),
        scratch_shapes=[
            pltpu.VMEM((2, 224, 2 * C), BF),
            pltpu.VMEM((2, ROWS, 2 * C), BF),
            pltpu.SemaphoreType.DMA((2, 3)),
            pltpu.SemaphoreType.DMA((2, 3)),
        ],
        compiler_params=pltpu.CompilerParams(collective_id=0, has_side_effects=True, vmem_limit_bytes=48 * 1024 * 1024),
    )(x, ct, pack, place0, place1)


def out_call(gi, red, unpack, unplace0, unplace1):
    return pl.pallas_call(
        out_kernel,
        out_shape=(jax.ShapeDtypeStruct((4, N, C), BF), jax.ShapeDtypeStruct((12, OFFS, N), F32)),
        in_specs=[VM] * 5,
        out_specs=(VM, VM),
        scratch_shapes=[
            pltpu.VMEM((2, ROWS, C), BF),
            pltpu.VMEM((2, ROWS, C), BF),
            pltpu.VMEM((7, 48, 128), BF),
            pltpu.VMEM((48, 128), BF),
            pltpu.VMEM((7, 48, 128), BF),
            pltpu.VMEM((48, 128), BF),
            pltpu.VMEM((8, 48, 128), BF),
            pltpu.SemaphoreType.DMA((2, 3)),
            pltpu.SemaphoreType.DMA((2, 3)),
            pltpu.SemaphoreType.DMA((3, 7)),
            pltpu.SemaphoreType.DMA((3, 7)),
        ],
        compiler_params=pltpu.CompilerParams(collective_id=1, has_side_effects=True, vmem_limit_bytes=48 * 1024 * 1024),
    )(gi, red, unpack, unplace0, unplace1)


def on_device(block_input, cotangent, first_gain, second_gain, input_weight, output_weight, up_weight,
              down_weight, bias_table):
    spread, pick = spread_consts()
    pack, place0, place1 = piece_consts()
    as_bf = lambda v: jnp.asarray(v, BF)
    xw, cw = in_call(block_input.reshape(4, N, C), cotangent.reshape(4, N, C), as_bf(pack), as_bf(place0), as_bf(place1))
    gi, red = main_call(xw, cw, first_gain[None], second_gain[None], input_weight, output_weight, up_weight,
                        down_weight, bias_table.reshape(12, OFFS, N), as_bf(spread), jnp.asarray(pick))
    gx, gb = out_call(gi, red, as_bf(pack.transpose(0, 2, 1)), as_bf(place0.T), as_bf(place1.T))
    return gx.reshape(block_input.shape), gb.reshape(bias_table.shape)


def solution(mesh):
    P = jax.sharding.PartitionSpec
    in_specs = (
        P(None, "lat", "lon", None),
        P(None, "lat", "lon", None),
        P(), P(), P(), P(), P(), P(),
        P(None, "lat", None, None, None),
    )
    out_specs = (P(None, "lat", "lon", None), P(None, "lat", None, None, None))
    return jax.shard_map(on_device, mesh=mesh, in_specs=in_specs, out_specs=out_specs, check_vma=False)
```

```python
import functools
import numpy as np
import jax
import jax.numpy as jnp
from jax import lax
from jax.experimental import pallas as pl
from jax.experimental.pallas import tpu as pltpu

BF = jnp.bfloat16
F32 = jnp.float32
HEADS, WZ, WH, WW = 6, 2, 6, 12
HD = 32
C = 192
FF = 768
N = 144
PS = WZ * WH
OFFS = 2 * WW - 1
LW = 384
EPS = 1e-05
SCALE = HD ** -0.5
NEG = -1e30
LOG2E = 1.4426950408889634


def nn(a, b):
    return lax.dot_general(a, b, (((1,), (0,)), ((), ())), preferred_element_type=F32)


def nt(a, b):
    return lax.dot_general(a, b, (((1,), (1,)), ((), ())), preferred_element_type=F32)


def tn(a, b):
    return lax.dot_general(a, b, (((0,), (0,)), ((), ())), preferred_element_type=F32)


def spread_consts():
    spread = np.zeros((N, PS, LW), np.float32)
    for p in range(WZ):
        for q in range(WZ):
            for s in range(WH):
                for t in range(WH):
                    m = ((p * WZ + q) * WH + s) * WH + t
                    for r in range(OFFS):
                        spread[m, q * WH + t, r * PS + p * WH + s] = 1
    pick = np.zeros((24, LW), np.float32)
    for r in range(OFFS):
        pick[r, r * PS:(r + 1) * PS] = 1
    return spread.reshape(N, PS * LW), pick


def normalize(v):
    centred = v - jnp.mean(v, axis=-1, keepdims=True)
    rs = lax.rsqrt(jnp.mean(centred * centred, axis=-1, keepdims=True) + EPS)
    return centred * rs, rs


def norm_back(g, xh, rs):
    return rs * (g - jnp.mean(g, axis=-1, keepdims=True) - xh * jnp.mean(g * xh, axis=-1, keepdims=True))


def gelu_slope(h):
    cdf = 0.5 + 0.5 * lax.erf(h * 0.7071067811865476)
    return cdf + h * (jnp.exp(-0.5 * (h * h)) * 0.3989422804014327)


def expand_bias(lat, spread_ref, pick_ref, t24, strips, bias):
    table = t24[...].reshape(12 * 24, N)
    hi = table.astype(BF)
    rest = table - hi.astype(F32)
    mid = rest.astype(BF)
    low = (rest - mid.astype(F32)).astype(BF)
    pick = pick_ref[...][None] * LOG2E
    for qt in range(PS):
        sel = spread_ref[:, qt * LW:(qt + 1) * LW]
        wide = nn(hi, sel) + nn(mid, sel) + nn(low, sel)
        strips[:, qt, :] = jnp.sum(wide.reshape(12, 24, LW) * pick, axis=1)
    row = lax.broadcasted_iota(jnp.int32, (N, N), 0).astype(F32)
    col = lax.broadcasted_iota(jnp.int32, (N, N), 1).astype(F32)

    def place(v):
        ps = v - PS * jnp.floor((v + 0.5) * (1.0 / PS))
        upper = (ps >= WH).astype(F32)
        s = ps - WH * upper
        return upper, (s >= WH // 2).astype(F32)

    rp, rs = place(row)
    cp, cs = place(col)
    last_band = (lat == 3).astype(F32)
    apart_rows = jnp.abs(rs - cs) * last_band
    apart_levels = jnp.abs(rp - cp)
    for a in range(2):
        apart = apart_rows + apart_levels if a else apart_rows
        excluded = jnp.where(apart > 0.5, NEG, 0.0)
        for an in range(a * HEADS, (a + 1) * HEADS):
            strip = strips[an, 0:PS, :]
            for j in range(WW):
                lo = (WW - 1 - j) * PS
                rows = slice(j * PS, (j + 1) * PS)
                bias[an, rows, :] = strip[:, lo:lo + N] + excluded[rows]


GROUPS = ((0, 4), (4, 6))


def zone_step(a, x, ct, g1, g2, wq, wk, wv, wqkvt, wo_ref, wu_ref, wdt_ref,
              bias, masked, probs, dscores, mixed, dbias, hooks=()):
    halves = (slice(0, N), slice(N, 2 * N))
    heads = [slice(n * HD, (n + 1) * HD) for n in range(HEADS)]
    lane = lax.broadcasted_iota(jnp.int32, (1, 128), 1)
    picks = [((lane >= n * HD % 128) & (lane < n * HD % 128 + HD)).astype(F32) for n in range(HEADS)]
    picks16 = [v.astype(BF) for v in picks]

    def by_head(c, v, kind):
        for n in range(HEADS):
            if n < 4:
                masked[kind, c, n * N:(n + 1) * N, :] = v[:, 0:128] * picks16[n]
            else:
                masked[kind, c, n * N:(n + 1) * N, 0:64] = v[:, 128:C] * picks16[n][:, 0:64]

    x = x.astype(F32)
    xh1, rs1 = normalize(x)
    xn1 = (xh1 * g1).astype(BF)
    queries = nn(xn1, wq[...]).astype(BF)
    keys = nn(xn1, wk[...]).astype(BF)
    values = nn(xn1, wv[...]).astype(BF)
    qkvt = [nt(wqkvt[...], xn1[halves[c]]).astype(BF) for c in range(2)]
    for c in range(2):
        by_head(c, keys[halves[c]], 0)
        by_head(c, values[halves[c]], 1)
    for first, end in GROUPS:
        width = min(C, end * HD) - first * HD
        for c in range(2):
            s_all = nn(masked[0, c, first * N:end * N, 0:width], qkvt[c][first * HD:end * HD, :])
            for n in range(first, end):
                s = s_all[(n - first) * N:(n - first + 1) * N] * (SCALE * LOG2E) + bias[a * HEADS + n]
                e = jnp.exp2(s - jnp.max(s, axis=0, keepdims=True))
                p = (e * (1.0 / jnp.sum(e, axis=0, keepdims=True))).astype(BF)
                probs[c, n * N:(n + 1) * N, :] = p
                mixed[c, heads[n], :] = nn(qkvt[c][2 * C + n * HD:2 * C + (n + 1) * HD], p).astype(BF)
    if "attended" in hooks:
        hooks["attended"]()
    attn = jnp.concatenate([tn(mixed[c], wo_ref[...]) for c in range(2)], axis=0).astype(BF)
    y = x + attn.astype(F32)
    xh2, rs2 = normalize(y)
    xn2 = (xh2 * g2).astype(BF)
    dxn2 = jnp.zeros((2 * N, C), F32)
    for f in range(FF // 256):
        up = wu_ref[:, f * 256:(f + 1) * 256]
        h = nn(xn2, up)
        da = nn(ct, wdt_ref[:, f * 256:(f + 1) * 256])
        dh = (da * gelu_slope(h)).astype(BF)
        dxn2 = dxn2 + nt(dh, up)
    dy = ct.astype(F32) + norm_back(dxn2 * g2, xh2, rs2)
    gattn = dy.astype(BF)
    if "tail" in hooks:
        hooks["tail"]()
    dmix = nt(gattn, wo_ref[...]).astype(BF)
    dmixt = [nt(wo_ref[...], gattn[halves[c]]).astype(BF) for c in range(2)]
    dqs, dks, dvs = [[], []], [[], []], [[], []]
    for first, end in GROUPS:
        width = min(C, end * HD) - first * HD
        span = slice(first * HD, first * HD + width)
        parts = [[], []]
        for c in range(2):
            dp_all = nn(masked[1, c, first * N:end * N, 0:width], dmixt[c][span, :])
            for n in range(first, end):
                dp = dp_all[(n - first) * N:(n - first + 1) * N]
                p = probs[c, n * N:(n + 1) * N, :].astype(F32)
                pd = p * dp
                ds = pd - p * jnp.sum(pd, axis=0, keepdims=True)
                parts[c].append(ds)
                dsb = ds.astype(BF)
                dscores[c, n * N:(n + 1) * N, :] = dsb
                dqs[c].append(nn(qkvt[c][C + n * HD:C + (n + 1) * HD], dsb))
            dk_all = nn(dscores[c, first * N:end * N, :], queries[halves[c], span])
            dv_all = nn(probs[c, first * N:end * N, :], dmix[halves[c], span])
            for store, full in ((dks, dk_all), (dvs, dv_all)):
                total = jnp.zeros((N, width), F32)
                for n in range(first, end):
                    total = total + full[(n - first) * N:(n - first + 1) * N] * picks[n][:, 0:width]
                store[c].append(total)
        for n in range(first, end):
            dbias[a * HEADS + n] = parts[0][n - first] + parts[1][n - first]
    if "scores" in hooks:
        hooks["scores"]()
    dq = jnp.concatenate([(jnp.concatenate(dqs[c], axis=0) * SCALE).astype(BF).T for c in range(2)], axis=0)
    dk = (jnp.concatenate([jnp.concatenate(dks[c], axis=1) for c in range(2)], axis=0) * SCALE).astype(BF)
    dv = jnp.concatenate([jnp.concatenate(dvs[c], axis=1) for c in range(2)], axis=0).astype(BF)
    dxn1 = nt(dq, wq[...]) + nt(dk, wk[...]) + nt(dv, wv[...])
    return (dy + norm_back(dxn1.astype(BF).astype(F32) * g1, xh1, rs1)).astype(BF)


def fold_bias(a, dbias, spread_ref, pick_ref, strips, folded):
    for n in range(HEADS):
        total = jnp.zeros((PS, LW), F32)
        for j in range(WW):
            lo = (WW - 1 - j) * PS
            total = total + jnp.pad(dbias[a * HEADS + n, j * PS:(j + 1) * PS, :], ((0, 0), (lo, LW - N - lo)))
        strips[n, 0:PS, :] = total
    pick = pick_ref[...][None]
    total = jnp.zeros((HEADS * 24, N), F32)
    for qt in range(PS):
        rows = strips[0:HEADS, qt, :][:, None, :] * pick
        total = total + nt(rows.reshape(HEADS * 24, LW).astype(BF), spread_ref[:, qt * LW:(qt + 1) * LW])
    folded[...] = total.reshape(HEADS, 24, N)


def pack_fold(folded, red):
    flat = [folded[n, :, 0:128] for n in range(HEADS)]
    tails = jnp.zeros((24, 128), F32)
    for n in range(HEADS):
        tail = jnp.concatenate([folded[n, :, 128:N], jnp.zeros((24, 112), F32)], axis=1)
        tails = tails + (pltpu.roll(tail, 16 * n, 1) if n else tail)
    rows = jnp.concatenate(flat + [tails, jnp.zeros((256 - 7 * 24, 128), F32)], axis=0)
    red[...] = rows.astype(BF).reshape(8, 32, 128)


def unpack_fold(a, full, gb_ref):
    rows = full[...].astype(F32).reshape(256, 128)
    for n in range(HEADS):
        gb_ref[a * HEADS + n, :, 0:128] = rows[n * 24:n * 24 + OFFS]
        gb_ref[a * HEADS + n, :, 128:N] = rows[HEADS * 24:HEADS * 24 + OFFS, 16 * n:16 * (n + 1)]


def prepare_weights(wi_ref, wit, wq, wk, wv):
    wit[...] = wi_ref[...].T
    for k, ref in enumerate((wq, wk, wv)):
        ref[...] = wi_ref[:, k * C:(k + 1) * C]


VM = pl.BlockSpec(memory_space=pltpu.VMEM)

MAIN_SCRATCH = [
    pltpu.VMEM((12, 24, N), F32),
    pltpu.VMEM((12, 16, LW), F32),
    pltpu.VMEM((12, N, N), F32),
    pltpu.VMEM((3 * C, C), BF),
    pltpu.VMEM((C, C), BF),
    pltpu.VMEM((C, C), BF),
    pltpu.VMEM((C, C), BF),
    pltpu.VMEM((2, 2, HEADS * N, 128), BF),
    pltpu.VMEM((2, HEADS * N, N), BF),
    pltpu.VMEM((2, HEADS * N, N), BF),
    pltpu.VMEM((2, C, N), BF),
    pltpu.VMEM((12, N, N), F32),
    pltpu.VMEM((HEADS, 24, N), F32),
]


PIECE0, PIECE1 = 80, 48
LAT0, LAT1, OWN1, LON1, DIAG1, ROWS = 80, 160, 208, 256, 304, 352
MESH = pl.DeviceIdType.MESH


def piece_consts():
    pack = np.zeros((2, ROWS, N), np.float32)
    place0 = np.zeros((N, LAT1), np.float32)
    place1 = np.zeros((N, ROWS - LAT1), np.float32)
    for p in range(2):
        for h in range(6):
            own = h >= 3
            s = h - 3 if own else h + 3
            for w in range(24):
                e = (w - 6) % 24
                if e < 12:
                    row = (0 if own else LAT0) + (e * 2 + p) * 3 + s % 3
                    place0[e * PS + p * WH + s, row] = 1
                else:
                    e -= 12
                    base = (OWN1 if own else LAT1) if e < 6 else (LON1 if own else DIAG1)
                    row = base + ((e % 6) * 2 + p) * 3 + s % 3
                    place1[e * PS + p * WH + s, row - LAT1] = 1
                pack[p, row, h * 24 + w] = 1
    return pack, place0, place1


def lat_lon():
    return lax.axis_index("lat"), lax.axis_index("lon")


def shifted(lat, lon, da, do):
    return lax.rem(lat + 4 + da, 4), lax.rem(lon + 64 + do, 64)


def in_copies(a, lat, lon, out_box, land, send_sem, recv_sem):
    plan = ((0, 128, LAT0, (-1, 0)), (128, 48, LON1, (0, -1)), (176, 48, DIAG1, (-1, -1)))
    return [
        pltpu.make_async_remote_copy(
            src_ref=out_box.at[a, pl.ds(start, size)],
            dst_ref=land.at[a, pl.ds(target, size)],
            send_sem=send_sem.at[a, k],
            recv_sem=recv_sem.at[a, k],
            device_id=shifted(lat, lon, *step),
            device_id_type=MESH,
        )
        for k, (start, size, target, step) in enumerate(plan)
    ]


def back_copies(a, lat, lon, box, land, send_sem, recv_sem):
    plan = ((LAT0, 128, (1, 0)), (LON1, 48, (0, 1)), (DIAG1, 48, (1, 1)))
    return [
        pltpu.make_async_remote_copy(
            src_ref=box.at[a, pl.ds(start, size)],
            dst_ref=land.at[a, pl.ds(start, size)],
            send_sem=send_sem.at[a, k],
            recv_sem=recv_sem.at[a, k],
            device_id=shifted(lat, lon, *step),
            device_id_type=MESH,
        )
        for k, (start, size, step) in enumerate(plan)
    ]


def deep_peer(lon, d):
    high, z, y = lon // 32, lax.rem(lon // 4, 8), lax.rem(lon, 4)
    return (high * 8 + lax.rem(z + d, 8)) * 4 + y


def flat_peer(lon, d):
    z = lax.rem(lon // 4, 8)
    place = lax.rem((lon // 32) * 4 + lax.rem(lon, 4) + d, 8)
    return ((place // 4) * 8 + z) * 4 + lax.rem(place, 4)


def sum_copies(kind, a, lat, lon, src, dst, send_sem, recv_sem):
    z = lax.rem(lon // 4, 8)
    copies = []
    for d in range(1, 8):
        if kind == 0:
            peer = deep_peer(lon, d)
            source, target = src.at[a, lax.rem(z + d, 8)], dst.at[a, d - 1]
        elif kind == 1:
            peer = flat_peer(lon, d)
            source, target = src.at[a], dst.at[a, d - 1]
        else:
            peer = deep_peer(lon, d)
            source, target = src.at[a], dst.at[a, z]
        copies.append(pltpu.make_async_remote_copy(
            src_ref=source, dst_ref=target, send_sem=send_sem.at[a, kind, d - 1], recv_sem=recv_sem.at[a, kind, d - 1],
            device_id=(lat, peer), device_id_type=MESH))
    return copies


def add_up(own, slots):
    total = own.astype(F32)
    for d in range(7):
        total = total + slots[d].astype(F32)
    return total.astype(BF)


LOCAL = (
    ((4, N, C), BF), ((4, N, C), BF), ((2, ROWS, N), BF), ((N, LAT1), BF), ((N, ROWS - LAT1), BF),
    ((12, OFFS, N), F32), ((1, C), F32), ((1, C), F32), ((C, 3 * C), BF), ((C, C), BF), ((C, FF), BF), ((C, FF), BF),
    ((N, PS * LW), BF), ((24, LW), F32), ((2, N, ROWS), BF), ((LAT1, N), BF), ((ROWS - LAT1, N), BF),
)


def block_kernel(*refs):
    count = len(LOCAL)
    far = refs[:count]
    gx_ref, gb_ref = refs[count:count + 2]
    near = refs[count + 2:2 * count + 2]
    (x_ref, ct_ref, pack_ref, place0_ref, place1_ref, tb_ref, g1_ref, g2_ref, wi_ref, wo_ref, wu_ref, wdt_ref,
     spread_ref, pick_ref, unpack_ref, unplace0_ref, unplace1_ref) = near
    (t24, strips, bias, wit, wq, wk, wv, masked, probs, dscores, mixed, dbias, folded,
     out_box, land, back_box, back_land, red, slots1, part, slots2, whole, full,
     near_sem, in_send, in_recv, back_send, back_recv, sum_send, sum_recv) = refs[2 * count + 2:]
    lat, lon = lat_lon()
    z = lax.rem(lon // 4, 8)

    barrier = pltpu.get_barrier_semaphore()
    for da, do in ((1, 0), (0, 1), (1, 1), (-1, 0), (0, -1), (-1, -1)):
        pl.semaphore_signal(barrier, inc=1, device_id=shifted(lat, lon, da, do), device_id_type=MESH)
    for d in range(1, 8):
        pl.semaphore_signal(barrier, inc=1, device_id=(lat, deep_peer(lon, d)), device_id_type=MESH)
        pl.semaphore_signal(barrier, inc=1, device_id=(lat, flat_peer(lon, d)), device_id_type=MESH)
    fetches = [pltpu.make_async_copy(far[k], near[k], near_sem.at[k]) for k in range(count)]
    for fetch in fetches:
        fetch.start()
    for fetch in fetches[0:3]:
        fetch.wait()

    arrivals = []
    for a in range(2):
        for k, ref in enumerate((x_ref, ct_ref)):
            piece = (nn(pack_ref[0], ref[(2 * a + 1) % 4]) + nn(pack_ref[1], ref[(2 * a + 2) % 4])).astype(BF)
            lanes = slice(k * C, (k + 1) * C)
            land[a, 0:LAT0, lanes] = piece[0:LAT0]
            land[a, OWN1:LON1, lanes] = piece[OWN1:LON1]
            out_box[a, 0:128, lanes] = piece[LAT0:OWN1]
            out_box[a, 128:224, lanes] = piece[LON1:ROWS]
        if a == 0:
            pl.semaphore_wait(barrier, 20)
        arrivals.append(in_copies(a, lat, lon, out_box, land, in_send, in_recv))
        for copy in arrivals[a]:
            copy.start()

    for fetch in fetches[3:]:
        fetch.wait()
    t24[...] = jnp.zeros_like(t24)
    t24[:, 0:OFFS, :] = tb_ref[...]
    prepare_weights(wi_ref, wit, wq, wk, wv)
    expand_bias(lat, spread_ref, pick_ref, t24, strips, bias)
    g1, g2 = g1_ref[...], g2_ref[...]

    sums = [[sum_copies(kind, a, lat, lon, src, dst, sum_send, sum_recv)
             for kind, (src, dst) in enumerate(((red, slots1), (part, slots2), (whole, full)))] for a in range(2)]

    def sum_first(a):
        fold_bias(a, dbias, spread_ref, pick_ref, strips, folded)
        pack_fold(folded, red.at[a])
        for copy in sums[a][0]:
            copy.start()

    def sum_second(a):
        for copy in sums[a][0]:
            copy.wait()
        part[a] = add_up(red[a, z], slots1.at[a])
        for copy in sums[a][1]:
            copy.start()

    def sum_third(a):
        for copy in sums[a][1]:
            copy.wait()
        whole[a] = add_up(part[a], slots2.at[a])
        for copy in sums[a][2]:
            copy.start()
        full[a, z] = whole[a]

    def sum_last(a):
        for copy in sums[a][2]:
            copy.wait()
        unpack_fold(a, full.at[a], gb_ref)

    def zone(a, hooks):
        for copy in arrivals[a]:
            copy.wait()
        first = nn(place0_ref[...], land[a, 0:LAT1, :]).astype(BF)
        second = nn(place1_ref[...], land[a, LAT1:ROWS, :]).astype(BF)
        xw = jnp.concatenate([first[:, 0:C], second[:, 0:C]], axis=0)
        cw = jnp.concatenate([first[:, C:], second[:, C:]], axis=0)
        gi = zone_step(a, xw, cw, g1, g2, wq, wk, wv, wit, wo_ref, wu_ref, wdt_ref,
                       bias, masked, probs, dscores, mixed, dbias, hooks)
        first = nn(unplace0_ref[...], gi[0:N]).astype(BF)
        second = nn(unplace1_ref[...], gi[N:]).astype(BF)
        back_land[a, 0:LAT0, :] = first[0:LAT0]
        back_land[a, OWN1:LON1, :] = second[OWN1 - LAT1:LON1 - LAT1]
        back_box[a, LAT0:LAT1, :] = first[LAT0:LAT1]
        back_box[a, LAT1:OWN1, :] = second[0:OWN1 - LAT1]
        back_box[a, LON1:ROWS, :] = second[LON1 - LAT1:]
        copies = back_copies(a, lat, lon, back_box, back_land, back_send, back_recv)
        for copy in copies:
            copy.start()
        return copies

    def collect(a, copies):
        for copy in copies:
            copy.wait()
        for p in range(2):
            gx_ref[(2 * a + 1 + p) % 4] = nn(unpack_ref[p], back_land[a]).astype(BF)

    back0 = zone(0, {"scores": lambda: sum_first(0)})
    back1 = zone(1, {"attended": lambda: sum_second(0), "tail": lambda: sum_third(0), "scores": lambda: sum_first(1)})
    collect(0, back0)
    sum_last(0)
    sum_second(1)
    collect(1, back1)
    sum_third(1)
    sum_last(1)


def block_call(*operands):
    anywhere = pl.BlockSpec(memory_space=pl.ANY)
    dma = pltpu.SemaphoreType.DMA
    return pl.pallas_call(
        block_kernel,
        out_shape=(jax.ShapeDtypeStruct((4, N, C), BF), jax.ShapeDtypeStruct((12, OFFS, N), F32)),
        in_specs=[anywhere] * len(LOCAL),
        out_specs=(VM, VM),
        scratch_shapes=[pltpu.VMEM(*one) for one in LOCAL] + MAIN_SCRATCH + [
            pltpu.VMEM((2, 224, 2 * C), BF),
            pltpu.VMEM((2, ROWS, 2 * C), BF),
            pltpu.VMEM((2, ROWS, C), BF),
            pltpu.VMEM((2, ROWS, C), BF),
            pltpu.VMEM((2, 8, 32, 128), BF),
            pltpu.VMEM((2, 7, 32, 128), BF),
            pltpu.VMEM((2, 32, 128), BF),
            pltpu.VMEM((2, 7, 32, 128), BF),
            pltpu.VMEM((2, 32, 128), BF),
            pltpu.VMEM((2, 8, 32, 128), BF),
            dma((len(LOCAL),)), dma((2, 3)), dma((2, 3)), dma((2, 3)), dma((2, 3)), dma((2, 3, 7)), dma((2, 3, 7)),
        ],
        compiler_params=pltpu.CompilerParams(collective_id=0, has_side_effects=True, vmem_limit_bytes=60 * 1024 * 1024),
    )(*operands)


def on_device(block_input, cotangent, first_gain, second_gain, input_weight, output_weight, up_weight,
              down_weight, bias_table):
    spread, pick = spread_consts()
    pack, place0, place1 = piece_consts()
    as_bf = lambda v: jnp.asarray(v, BF)
    gx, gb = block_call(
        block_input.reshape(4, N, C), cotangent.reshape(4, N, C), as_bf(pack), as_bf(place0), as_bf(place1),
        bias_table.reshape(12, OFFS, N),
        first_gain[None], second_gain[None], input_weight, output_weight, up_weight, down_weight.T,
        as_bf(spread), jnp.asarray(pick), as_bf(pack.transpose(0, 2, 1)), as_bf(place0.T), as_bf(place1.T))
    return gx.reshape(block_input.shape), gb.reshape(bias_table.shape)


def solution(mesh):
    P = jax.sharding.PartitionSpec
    in_specs = (
        P(None, "lat", "lon", None),
        P(None, "lat", "lon", None),
        P(), P(), P(), P(), P(), P(),
        P(None, "lat", None, None, None),
    )
    out_specs = (P(None, "lat", "lon", None), P(None, "lat", None, None, None))
    return jax.shard_map(on_device, mesh=mesh, in_specs=in_specs, out_specs=out_specs, check_vma=False)
```

```python
import functools
import numpy as np
import jax
import jax.numpy as jnp
from jax import lax
from jax.experimental import pallas as pl
from jax.experimental.pallas import tpu as pltpu

BF = jnp.bfloat16
F32 = jnp.float32
HEADS, WZ, WH, WW = 6, 2, 6, 12
HD = 32
C = 192
FF = 768
N = 144
PS = WZ * WH
OFFS = 2 * WW - 1
LW = 384
EPS = 1e-05
SCALE = HD ** -0.5
NEG = -1e30
LOG2E = 1.4426950408889634


def nn(a, b):
    return lax.dot_general(a, b, (((1,), (0,)), ((), ())), preferred_element_type=F32)


def nt(a, b):
    return lax.dot_general(a, b, (((1,), (1,)), ((), ())), preferred_element_type=F32)


def tn(a, b):
    return lax.dot_general(a, b, (((0,), (0,)), ((), ())), preferred_element_type=F32)


def spread_consts():
    spread = np.zeros((N, PS, LW), np.float32)
    for p in range(WZ):
        for q in range(WZ):
            for s in range(WH):
                for t in range(WH):
                    m = ((p * WZ + q) * WH + s) * WH + t
                    for r in range(OFFS):
                        spread[m, q * WH + t, r * PS + p * WH + s] = 1
    pick = np.zeros((24, LW), np.float32)
    for r in range(OFFS):
        pick[r, r * PS:(r + 1) * PS] = 1
    return spread.reshape(N, PS * LW), pick


def normalize(v):
    centred = v - jnp.mean(v, axis=-1, keepdims=True)
    rs = lax.rsqrt(jnp.mean(centred * centred, axis=-1, keepdims=True) + EPS)
    return centred * rs, rs


def norm_back(g, xh, rs):
    return rs * (g - jnp.mean(g, axis=-1, keepdims=True) - xh * jnp.mean(g * xh, axis=-1, keepdims=True))


def gelu_slope(h):
    cdf = 0.5 + 0.5 * lax.erf(h * 0.7071067811865476)
    return cdf + h * (jnp.exp(-0.5 * (h * h)) * 0.3989422804014327)


def expand_bias(lat, spread_ref, pick_ref, t24, strips, bias):
    table = t24[...].reshape(12 * 24, N)
    hi = table.astype(BF)
    rest = table - hi.astype(F32)
    mid = rest.astype(BF)
    low = (rest - mid.astype(F32)).astype(BF)
    pick = pick_ref[...][None] * LOG2E
    for qt in range(PS):
        sel = spread_ref[:, qt * LW:(qt + 1) * LW]
        wide = nn(hi, sel) + nn(mid, sel) + nn(low, sel)
        strips[:, qt, :] = jnp.sum(wide.reshape(12, 24, LW) * pick, axis=1)
    row = lax.broadcasted_iota(jnp.int32, (N, N), 0).astype(F32)
    col = lax.broadcasted_iota(jnp.int32, (N, N), 1).astype(F32)

    def place(v):
        ps = v - PS * jnp.floor((v + 0.5) * (1.0 / PS))
        upper = (ps >= WH).astype(F32)
        s = ps - WH * upper
        return upper, (s >= WH // 2).astype(F32)

    rp, rs = place(row)
    cp, cs = place(col)
    last_band = (lat == 3).astype(F32)
    apart_rows = jnp.abs(rs - cs) * last_band
    apart_levels = jnp.abs(rp - cp)
    for a in range(2):
        apart = apart_rows + apart_levels if a else apart_rows
        excluded = jnp.where(apart > 0.5, NEG, 0.0)
        for an in range(a * HEADS, (a + 1) * HEADS):
            strip = strips[an, 0:PS, :]
            for j in range(WW):
                lo = (WW - 1 - j) * PS
                rows = slice(j * PS, (j + 1) * PS)
                bias[an, rows, :] = strip[:, lo:lo + N] + excluded[rows]


GROUPS = ((0, 4), (4, 6))


def halves():
    return slice(0, N), slice(N, 2 * N)


def head_picks():
    lane = lax.broadcasted_iota(jnp.int32, (1, 128), 1)
    return [((lane >= n * HD % 128) & (lane < n * HD % 128 + HD)).astype(F32) for n in range(HEADS)]


def zone_scores(a, x, ct, g1, g2, wq, wk, wv, wqkvt, wo_ref, wu_ref, wdt_ref,
                bias, masked, probs, dscores, mixed, dbias):
    half = halves()
    picks16 = [v.astype(BF) for v in head_picks()]

    def by_head(c, v, kind):
        for n in range(HEADS):
            if n < 4:
                masked[kind, c, n * N:(n + 1) * N, :] = v[:, 0:128] * picks16[n]
            else:
                masked[kind, c, n * N:(n + 1) * N, 0:64] = v[:, 128:C] * picks16[n][:, 0:64]

    x = x.astype(F32)
    xh1, rs1 = normalize(x)
    xn1 = (xh1 * g1).astype(BF)
    keys = nn(xn1, wk[...]).astype(BF)
    values = nn(xn1, wv[...]).astype(BF)
    qkvt = [nt(wqkvt[...], xn1[half[c]]).astype(BF) for c in range(2)]
    for c in range(2):
        by_head(c, keys[half[c]], 0)
        by_head(c, values[half[c]], 1)
    for first, end in GROUPS:
        width = min(C, end * HD) - first * HD
        for c in range(2):
            s_all = nn(masked[0, c, first * N:end * N, 0:width], qkvt[c][first * HD:end * HD, :])
            for n in range(first, end):
                s = s_all[(n - first) * N:(n - first + 1) * N] * (SCALE * LOG2E) + bias[a * HEADS + n]
                e = jnp.exp2(s - jnp.max(s, axis=0, keepdims=True))
                p = (e * (1.0 / jnp.sum(e, axis=0, keepdims=True))).astype(BF)
                probs[c, n * N:(n + 1) * N, :] = p
                mixed[c, n * HD:(n + 1) * HD, :] = nn(qkvt[c][2 * C + n * HD:2 * C + (n + 1) * HD], p).astype(BF)
    attn = jnp.concatenate([tn(mixed[c], wo_ref[...]) for c in range(2)], axis=0).astype(BF)
    y = x + attn.astype(F32)
    xh2, rs2 = normalize(y)
    xn2 = (xh2 * g2).astype(BF)
    dxn2 = jnp.zeros((2 * N, C), F32)
    for f in range(FF // 256):
        up = wu_ref[:, f * 256:(f + 1) * 256]
        h = nn(xn2, up)
        da = nn(ct, wdt_ref[:, f * 256:(f + 1) * 256])
        dh = (da * gelu_slope(h)).astype(BF)
        dxn2 = dxn2 + nt(dh, up)
    dy = ct.astype(F32) + norm_back(dxn2 * g2, xh2, rs2)
    gattn = dy.astype(BF)
    dmixt = [nt(wo_ref[...], gattn[half[c]]).astype(BF) for c in range(2)]
    for first, end in GROUPS:
        width = min(C, end * HD) - first * HD
        span = slice(first * HD, first * HD + width)
        parts = [[], []]
        for c in range(2):
            dp_all = nn(masked[1, c, first * N:end * N, 0:width], dmixt[c][span, :])
            for n in range(first, end):
                dp = dp_all[(n - first) * N:(n - first + 1) * N]
                p = probs[c, n * N:(n + 1) * N, :].astype(F32)
                pd = p * dp
                ds = pd - p * jnp.sum(pd, axis=0, keepdims=True)
                parts[c].append(ds)
                dscores[c, n * N:(n + 1) * N, :] = ds.astype(BF)
        for n in range(first, end):
            dbias[a * HEADS + n] = parts[0][n - first] + parts[1][n - first]
    return xh1, rs1, xn1, [v[C:2 * C] for v in qkvt], dy, gattn


def zone_finish(state, g1, wq, wk, wv, wo_ref, probs, dscores):
    half = halves()
    picks = head_picks()
    xh1, rs1, xn1, keyst, dy, gattn = state
    queries = nn(xn1, wq[...]).astype(BF)
    dmix = nt(gattn, wo_ref[...]).astype(BF)
    dqs, dks, dvs = [[], []], [[], []], [[], []]
    for first, end in GROUPS:
        width = min(C, end * HD) - first * HD
        span = slice(first * HD, first * HD + width)
        for c in range(2):
            for n in range(first, end):
                dqs[c].append(nn(keyst[c][n * HD:(n + 1) * HD], dscores[c, n * N:(n + 1) * N, :]))
            dk_all = nn(dscores[c, first * N:end * N, :], queries[half[c], span])
            dv_all = nn(probs[c, first * N:end * N, :], dmix[half[c], span])
            for store, full in ((dks, dk_all), (dvs, dv_all)):
                total = jnp.zeros((N, width), F32)
                for n in range(first, end):
                    total = total + full[(n - first) * N:(n - first + 1) * N] * picks[n][:, 0:width]
                store[c].append(total)
    dq = jnp.concatenate([(jnp.concatenate(dqs[c], axis=0) * SCALE).astype(BF).T for c in range(2)], axis=0)
    dk = (jnp.concatenate([jnp.concatenate(dks[c], axis=1) for c in range(2)], axis=0) * SCALE).astype(BF)
    dv = jnp.concatenate([jnp.concatenate(dvs[c], axis=1) for c in range(2)], axis=0).astype(BF)
    dxn1 = nt(dq, wq[...]) + nt(dk, wk[...]) + nt(dv, wv[...])
    return (dy + norm_back(dxn1.astype(BF).astype(F32) * g1, xh1, rs1)).astype(BF)


def fold_bias(a, dbias, spread_ref, pick_ref, strips, folded):
    for n in range(HEADS):
        total = jnp.zeros((PS, LW), F32)
        for j in range(WW):
            lo = (WW - 1 - j) * PS
            total = total + jnp.pad(dbias[a * HEADS + n, j * PS:(j + 1) * PS, :], ((0, 0), (lo, LW - N - lo)))
        strips[n, 0:PS, :] = total
    pick = pick_ref[...][None]
    total = jnp.zeros((HEADS * 24, N), F32)
    for qt in range(PS):
        rows = strips[0:HEADS, qt, :][:, None, :] * pick
        total = total + nt(rows.reshape(HEADS * 24, LW).astype(BF), spread_ref[:, qt * LW:(qt + 1) * LW])
    folded[...] = total.reshape(HEADS, 24, N)


def pack_fold(folded, red):
    flat = [folded[n, :, 0:128] for n in range(HEADS)]
    tails = jnp.zeros((24, 128), F32)
    for n in range(HEADS):
        tail = jnp.concatenate([folded[n, :, 128:N], jnp.zeros((24, 112), F32)], axis=1)
        tails = tails + (pltpu.roll(tail, 16 * n, 1) if n else tail)
    rows = jnp.concatenate(flat + [tails, jnp.zeros((256 - 7 * 24, 128), F32)], axis=0)
    red[...] = rows.astype(BF).reshape(8, 32, 128)


def unpack_fold(a, full, gb_ref):
    rows = full[...].astype(F32).reshape(256, 128)
    for n in range(HEADS):
        gb_ref[a * HEADS + n, :, 0:128] = rows[n * 24:n * 24 + OFFS]
        gb_ref[a * HEADS + n, :, 128:N] = rows[HEADS * 24:HEADS * 24 + OFFS, 16 * n:16 * (n + 1)]


def prepare_weights(wi_ref, wit, wq, wk, wv):
    wit[...] = wi_ref[...].T
    for k, ref in enumerate((wq, wk, wv)):
        ref[...] = wi_ref[:, k * C:(k + 1) * C]


VM = pl.BlockSpec(memory_space=pltpu.VMEM)

MAIN_SCRATCH = [
    pltpu.VMEM((12, 24, N), F32),
    pltpu.VMEM((12, 16, LW), F32),
    pltpu.VMEM((12, N, N), F32),
    pltpu.VMEM((3 * C, C), BF),
    pltpu.VMEM((C, C), BF),
    pltpu.VMEM((C, C), BF),
    pltpu.VMEM((C, C), BF),
    pltpu.VMEM((2, 2, 2, HEADS * N, 128), BF),
    pltpu.VMEM((2, 2, HEADS * N, N), BF),
    pltpu.VMEM((2, 2, HEADS * N, N), BF),
    pltpu.VMEM((2, 2, C, N), BF),
    pltpu.VMEM((12, N, N), F32),
    pltpu.VMEM((HEADS, 24, N), F32),
]


PIECE0, PIECE1 = 80, 48
LAT0, LAT1, OWN1, LON1, DIAG1, ROWS = 80, 160, 208, 256, 304, 352
MESH = pl.DeviceIdType.MESH


def piece_consts():
    pack = np.zeros((2, ROWS, N), np.float32)
    place0 = np.zeros((N, LAT1), np.float32)
    place1 = np.zeros((N, ROWS - LAT1), np.float32)
    for p in range(2):
        for h in range(6):
            own = h >= 3
            s = h - 3 if own else h + 3
            for w in range(24):
                e = (w - 6) % 24
                if e < 12:
                    row = (0 if own else LAT0) + (e * 2 + p) * 3 + s % 3
                    place0[e * PS + p * WH + s, row] = 1
                else:
                    e -= 12
                    base = (OWN1 if own else LAT1) if e < 6 else (LON1 if own else DIAG1)
                    row = base + ((e % 6) * 2 + p) * 3 + s % 3
                    place1[e * PS + p * WH + s, row - LAT1] = 1
                pack[p, row, h * 24 + w] = 1
    return pack, place0, place1


def lat_lon():
    return lax.axis_index("lat"), lax.axis_index("lon")


def shifted(lat, lon, da, do):
    return lax.rem(lat + 4 + da, 4), lax.rem(lon + 64 + do, 64)


def in_copies(a, lat, lon, out_box, land, send_sem, recv_sem):
    plan = ((0, 128, LAT0, (-1, 0)), (128, 48, LON1, (0, -1)), (176, 48, DIAG1, (-1, -1)))
    return [
        pltpu.make_async_remote_copy(
            src_ref=out_box.at[a, pl.ds(start, size)],
            dst_ref=land.at[a, pl.ds(target, size)],
            send_sem=send_sem.at[a, k],
            recv_sem=recv_sem.at[a, k],
            device_id=shifted(lat, lon, *step),
            device_id_type=MESH,
        )
        for k, (start, size, target, step) in enumerate(plan)
    ]


def back_copies(a, lat, lon, box, land, send_sem, recv_sem):
    plan = ((LAT0, 128, (1, 0)), (LON1, 48, (0, 1)), (DIAG1, 48, (1, 1)))
    return [
        pltpu.make_async_remote_copy(
            src_ref=box.at[a, pl.ds(start, size)],
            dst_ref=land.at[a, pl.ds(start, size)],
            send_sem=send_sem.at[a, k],
            recv_sem=recv_sem.at[a, k],
            device_id=shifted(lat, lon, *step),
            device_id_type=MESH,
        )
        for k, (start, size, step) in enumerate(plan)
    ]


def deep_peer(lon, d):
    high, z, y = lon // 32, lax.rem(lon // 4, 8), lax.rem(lon, 4)
    return (high * 8 + lax.rem(z + d, 8)) * 4 + y


def flat_peer(lon, d):
    z = lax.rem(lon // 4, 8)
    place = lax.rem((lon // 32) * 4 + lax.rem(lon, 4) + d, 8)
    return ((place // 4) * 8 + z) * 4 + lax.rem(place, 4)


def sum_copies(kind, a, lat, lon, src, dst, send_sem, recv_sem):
    z = lax.rem(lon // 4, 8)
    copies = []
    for d in range(1, 8):
        if kind == 0:
            peer = deep_peer(lon, d)
            source, target = src.at[a, lax.rem(z + d, 8)], dst.at[a, d - 1]
        elif kind == 1:
            peer = flat_peer(lon, d)
            source, target = src.at[a], dst.at[a, d - 1]
        else:
            peer = deep_peer(lon, d)
            source, target = src.at[a], dst.at[a, z]
        copies.append(pltpu.make_async_remote_copy(
            src_ref=source, dst_ref=target, send_sem=send_sem.at[a, kind, d - 1], recv_sem=recv_sem.at[a, kind, d - 1],
            device_id=(lat, peer), device_id_type=MESH))
    return copies


def add_up(own, slots):
    total = own.astype(F32)
    for d in range(7):
        total = total + slots[d].astype(F32)
    return total.astype(BF)


LOCAL = (
    ((4, N, C), BF), ((4, N, C), BF), ((2, ROWS, N), BF), ((N, LAT1), BF), ((N, ROWS - LAT1), BF),
    ((12, OFFS, N), F32), ((1, C), F32), ((1, C), F32), ((C, 3 * C), BF), ((C, C), BF), ((C, FF), BF), ((C, FF), BF),
    ((N, PS * LW), BF), ((24, LW), F32), ((2, N, ROWS), BF), ((LAT1, N), BF), ((ROWS - LAT1, N), BF),
)


def block_kernel(*refs):
    count = len(LOCAL)
    far = refs[:count]
    gx_ref, gb_ref = refs[count:count + 2]
    near = refs[count + 2:2 * count + 2]
    (x_ref, ct_ref, pack_ref, place0_ref, place1_ref, tb_ref, g1_ref, g2_ref, wi_ref, wo_ref, wu_ref, wdt_ref,
     spread_ref, pick_ref, unpack_ref, unplace0_ref, unplace1_ref) = near
    (t24, strips, bias, wit, wq, wk, wv, masked, probs, dscores, mixed, dbias, folded,
     out_box, land, back_box, back_land, red, slots1, part, slots2, whole, full,
     near_sem, in_send, in_recv, back_send, back_recv, sum_send, sum_recv) = refs[2 * count + 2:]
    lat, lon = lat_lon()
    z = lax.rem(lon // 4, 8)

    barrier = pltpu.get_barrier_semaphore()
    for da, do in ((1, 0), (0, 1), (1, 1), (-1, 0), (0, -1), (-1, -1)):
        pl.semaphore_signal(barrier, inc=1, device_id=shifted(lat, lon, da, do), device_id_type=MESH)
    for d in range(1, 8):
        pl.semaphore_signal(barrier, inc=1, device_id=(lat, deep_peer(lon, d)), device_id_type=MESH)
        pl.semaphore_signal(barrier, inc=1, device_id=(lat, flat_peer(lon, d)), device_id_type=MESH)
    fetches = [pltpu.make_async_copy(far[k], near[k], near_sem.at[k]) for k in range(count)]
    for fetch in fetches:
        fetch.start()
    for fetch in fetches[0:3]:
        fetch.wait()

    arrivals = []
    for a in range(2):
        for k, ref in enumerate((x_ref, ct_ref)):
            piece = (nn(pack_ref[0], ref[(2 * a + 1) % 4]) + nn(pack_ref[1], ref[(2 * a + 2) % 4])).astype(BF)
            lanes = slice(k * C, (k + 1) * C)
            land[a, 0:LAT0, lanes] = piece[0:LAT0]
            land[a, OWN1:LON1, lanes] = piece[OWN1:LON1]
            out_box[a, 0:128, lanes] = piece[LAT0:OWN1]
            out_box[a, 128:224, lanes] = piece[LON1:ROWS]
        if a == 0:
            pl.semaphore_wait(barrier, 20)
        arrivals.append(in_copies(a, lat, lon, out_box, land, in_send, in_recv))
        for copy in arrivals[a]:
            copy.start()

    for fetch in fetches[3:]:
        fetch.wait()
    t24[...] = jnp.zeros_like(t24)
    t24[:, 0:OFFS, :] = tb_ref[...]
    prepare_weights(wi_ref, wit, wq, wk, wv)
    expand_bias(lat, spread_ref, pick_ref, t24, strips, bias)
    g1, g2 = g1_ref[...], g2_ref[...]

    sums = [[sum_copies(kind, a, lat, lon, src, dst, sum_send, sum_recv)
             for kind, (src, dst) in enumerate(((red, slots1), (part, slots2), (whole, full)))] for a in range(2)]

    def sum_first(a):
        fold_bias(a, dbias, spread_ref, pick_ref, strips, folded)
        pack_fold(folded, red.at[a])
        for copy in sums[a][0]:
            copy.start()

    def sum_second(a):
        for copy in sums[a][0]:
            copy.wait()
        part[a] = add_up(red[a, z], slots1.at[a])
        for copy in sums[a][1]:
            copy.start()

    def sum_third(a):
        for copy in sums[a][1]:
            copy.wait()
        whole[a] = add_up(part[a], slots2.at[a])
        for copy in sums[a][2]:
            copy.start()
        full[a, z] = whole[a]

    def sum_last(a):
        for copy in sums[a][2]:
            copy.wait()
        unpack_fold(a, full.at[a], gb_ref)

    def begin(a):
        for copy in arrivals[a]:
            copy.wait()
        first = nn(place0_ref[...], land[a, 0:LAT1, :]).astype(BF)
        second = nn(place1_ref[...], land[a, LAT1:ROWS, :]).astype(BF)
        xw = jnp.concatenate([first[:, 0:C], second[:, 0:C]], axis=0)
        cw = jnp.concatenate([first[:, C:], second[:, C:]], axis=0)
        return zone_scores(a, xw, cw, g1, g2, wq, wk, wv, wit, wo_ref, wu_ref, wdt_ref, bias,
                           masked.at[a], probs.at[a], dscores.at[a], mixed.at[a], dbias)

    def finish(a, state):
        gi = zone_finish(state, g1, wq, wk, wv, wo_ref, probs.at[a], dscores.at[a])
        first = nn(unplace0_ref[...], gi[0:N]).astype(BF)
        second = nn(unplace1_ref[...], gi[N:]).astype(BF)
        back_land[a, 0:LAT0, :] = first[0:LAT0]
        back_land[a, OWN1:LON1, :] = second[OWN1 - LAT1:LON1 - LAT1]
        back_box[a, LAT0:LAT1, :] = first[LAT0:LAT1]
        back_box[a, LAT1:OWN1, :] = second[0:OWN1 - LAT1]
        back_box[a, LON1:ROWS, :] = second[LON1 - LAT1:]
        copies = back_copies(a, lat, lon, back_box, back_land, back_send, back_recv)
        for copy in copies:
            copy.start()
        return copies

    def collect(a, copies):
        for copy in copies:
            copy.wait()
        for p in range(2):
            gx_ref[(2 * a + 1 + p) % 4] = nn(unpack_ref[p], back_land[a]).astype(BF)

    state0 = begin(0)
    sum_first(0)
    state1 = begin(1)
    sum_first(1)
    sum_second(0)
    back0 = finish(0, state0)
    back1 = finish(1, state1)
    sum_second(1)
    sum_third(0)
    collect(0, back0)
    collect(1, back1)
    sum_third(1)
    sum_last(0)
    sum_last(1)


def block_call(*operands):
    anywhere = pl.BlockSpec(memory_space=pl.ANY)
    dma = pltpu.SemaphoreType.DMA
    return pl.pallas_call(
        block_kernel,
        out_shape=(jax.ShapeDtypeStruct((4, N, C), BF), jax.ShapeDtypeStruct((12, OFFS, N), F32)),
        in_specs=[anywhere] * len(LOCAL),
        out_specs=(VM, VM),
        scratch_shapes=[pltpu.VMEM(*one) for one in LOCAL] + MAIN_SCRATCH + [
            pltpu.VMEM((2, 224, 2 * C), BF),
            pltpu.VMEM((2, ROWS, 2 * C), BF),
            pltpu.VMEM((2, ROWS, C), BF),
            pltpu.VMEM((2, ROWS, C), BF),
            pltpu.VMEM((2, 8, 32, 128), BF),
            pltpu.VMEM((2, 7, 32, 128), BF),
            pltpu.VMEM((2, 32, 128), BF),
            pltpu.VMEM((2, 7, 32, 128), BF),
            pltpu.VMEM((2, 32, 128), BF),
            pltpu.VMEM((2, 8, 32, 128), BF),
            dma((len(LOCAL),)), dma((2, 3)), dma((2, 3)), dma((2, 3)), dma((2, 3)), dma((2, 3, 7)), dma((2, 3, 7)),
        ],
        compiler_params=pltpu.CompilerParams(collective_id=0, has_side_effects=True, vmem_limit_bytes=60 * 1024 * 1024),
    )(*operands)


def on_device(block_input, cotangent, first_gain, second_gain, input_weight, output_weight, up_weight,
              down_weight, bias_table):
    spread, pick = spread_consts()
    pack, place0, place1 = piece_consts()
    as_bf = lambda v: jnp.asarray(v, BF)
    gx, gb = block_call(
        block_input.reshape(4, N, C), cotangent.reshape(4, N, C), as_bf(pack), as_bf(place0), as_bf(place1),
        bias_table.reshape(12, OFFS, N),
        first_gain[None], second_gain[None], input_weight, output_weight, up_weight, down_weight.T,
        as_bf(spread), jnp.asarray(pick), as_bf(pack.transpose(0, 2, 1)), as_bf(place0.T), as_bf(place1.T))
    return gx.reshape(block_input.shape), gb.reshape(bias_table.shape)


def solution(mesh):
    P = jax.sharding.PartitionSpec
    in_specs = (
        P(None, "lat", "lon", None),
        P(None, "lat", "lon", None),
        P(), P(), P(), P(), P(), P(),
        P(None, "lat", None, None, None),
    )
    out_specs = (P(None, "lat", "lon", None), P(None, "lat", None, None, None))
    return jax.shard_map(on_device, mesh=mesh, in_specs=in_specs, out_specs=out_specs, check_vma=False)
```

```python
import functools
import numpy as np
import jax
import jax.numpy as jnp
from jax import lax
from jax.experimental import pallas as pl
from jax.experimental.pallas import tpu as pltpu

BF = jnp.bfloat16
F32 = jnp.float32
HEADS, WZ, WH, WW = 6, 2, 6, 12
HD = 32
C = 192
FF = 768
N = 144
PS = WZ * WH
OFFS = 2 * WW - 1
LW = 384
EPS = 1e-05
SCALE = HD ** -0.5
NEG = -1e30
LOG2E = 1.4426950408889634


def nn(a, b):
    return lax.dot_general(a, b, (((1,), (0,)), ((), ())), preferred_element_type=F32)


def nt(a, b):
    return lax.dot_general(a, b, (((1,), (1,)), ((), ())), preferred_element_type=F32)


def tn(a, b):
    return lax.dot_general(a, b, (((0,), (0,)), ((), ())), preferred_element_type=F32)


def fold_consts():
    join = np.zeros((LW, N), np.float32)
    own = np.zeros((16, N), np.float32)
    for p in range(WZ):
        for q in range(WZ):
            for s in range(WH):
                for t in range(WH):
                    m = ((p * WZ + q) * WH + s) * WH + t
                    own[q * WH + t, m] = 1
                    join[p * WH + s:OFFS * PS:PS, m] = 1
    pick = np.zeros((24, LW), np.float32)
    for r in range(OFFS):
        pick[r, r * PS:(r + 1) * PS] = 1
    return join, own, pick


def normalize(v):
    centred = v - jnp.mean(v, axis=-1, keepdims=True)
    rs = lax.rsqrt(jnp.mean(centred * centred, axis=-1, keepdims=True) + EPS)
    return centred * rs, rs


def norm_back(g, xh, rs):
    return rs * (g - jnp.mean(g, axis=-1, keepdims=True) - xh * jnp.mean(g * xh, axis=-1, keepdims=True))


def gelu_slope(h):
    cdf = 0.5 + 0.5 * lax.erf(h * 0.7071067811865476)
    return cdf + h * (jnp.exp(-0.5 * (h * h)) * 0.3989422804014327)


def expand_bias(lat, joint_ref, own_ref, pick_ref, t24, strips, bias):
    table = t24[...].reshape(12 * 24, N)
    hi = table.astype(BF)
    rest = table - hi.astype(F32)
    mid = rest.astype(BF)
    low = (rest - mid.astype(F32)).astype(BF)
    pick = pick_ref[...][None] * LOG2E
    for qt in range(PS):
        own = own_ref[qt:qt + 1, :]
        wide = nn(hi * own, joint_ref[...]) + nn(mid * own, joint_ref[...]) + nn(low * own, joint_ref[...])
        strips[:, qt, :] = jnp.sum(wide.reshape(12, 24, LW) * pick, axis=1)
    row = lax.broadcasted_iota(jnp.int32, (N, N), 0).astype(F32)
    col = lax.broadcasted_iota(jnp.int32, (N, N), 1).astype(F32)

    def place(v):
        ps = v - PS * jnp.floor((v + 0.5) * (1.0 / PS))
        upper = (ps >= WH).astype(F32)
        s = ps - WH * upper
        return upper, (s >= WH // 2).astype(F32)

    rp, rs = place(row)
    cp, cs = place(col)
    last_band = (lat == 3).astype(F32)
    apart_rows = jnp.abs(rs - cs) * last_band
    apart_levels = jnp.abs(rp - cp)
    for a in range(2):
        apart = apart_rows + apart_levels if a else apart_rows
        excluded = jnp.where(apart > 0.5, NEG, 0.0)
        for an in range(a * HEADS, (a + 1) * HEADS):
            strip = strips[an, 0:PS, :]
            for j in range(WW):
                lo = (WW - 1 - j) * PS
                rows = slice(j * PS, (j + 1) * PS)
                bias[an, rows, :] = strip[:, lo:lo + N] + excluded[rows]


GROUPS = ((0, 4), (4, 6))


def head_picks():
    lane = lax.broadcasted_iota(jnp.int32, (1, 128), 1)
    return [((lane >= n * HD % 128) & (lane < n * HD % 128 + HD)).astype(F32) for n in range(HEADS)]


WINDOWS = [slice(w * N, (w + 1) * N) for w in range(4)]


def all_scores(x, late_ct, g1, g2, wq, wk, wv, wqkvt, wo_ref, wu_ref, wdt_ref,
               bias, masked, probs, dscores, mixed, dbias, after_group):
    picks16 = [v.astype(BF) for v in head_picks()]

    def by_head(w, v, kind):
        for n in range(HEADS):
            if n < 4:
                masked[kind, w, n * N:(n + 1) * N, :] = v[:, 0:128] * picks16[n]
            else:
                masked[kind, w, n * N:(n + 1) * N, 0:64] = v[:, 128:C] * picks16[n][:, 0:64]

    x = x.astype(F32)
    xh1, rs1 = normalize(x)
    xn1 = (xh1 * g1).astype(BF)
    keys = nn(xn1, wk[...]).astype(BF)
    values = nn(xn1, wv[...]).astype(BF)
    qkvt = [nt(wqkvt[...], xn1[rows]).astype(BF) for rows in WINDOWS]
    for w, rows in enumerate(WINDOWS):
        by_head(w, keys[rows], 0)
        by_head(w, values[rows], 1)
    for first, end in GROUPS:
        width = min(C, end * HD) - first * HD
        for w in range(4):
            s_all = nn(masked[0, w, first * N:end * N, 0:width], qkvt[w][first * HD:end * HD, :])
            for n in range(first, end):
                s = s_all[(n - first) * N:(n - first + 1) * N] * (SCALE * LOG2E) + bias[(w // 2) * HEADS + n]
                e = jnp.exp2(s - jnp.max(s, axis=0, keepdims=True))
                p = (e * (1.0 / jnp.sum(e, axis=0, keepdims=True))).astype(BF)
                probs[w, n * N:(n + 1) * N, :] = p
                mixed[w, n * HD:(n + 1) * HD, :] = nn(qkvt[w][2 * C + n * HD:2 * C + (n + 1) * HD], p).astype(BF)
    ct = late_ct()
    attn = jnp.concatenate([tn(mixed[w], wo_ref[...]) for w in range(4)], axis=0).astype(BF)
    y = x + attn.astype(F32)
    xh2, rs2 = normalize(y)
    xn2 = (xh2 * g2).astype(BF)
    dxn2 = jnp.zeros((4 * N, C), F32)
    for f in range(FF // 256):
        up = wu_ref[:, f * 256:(f + 1) * 256]
        h = nn(xn2, up)
        da = nn(ct, wdt_ref[:, f * 256:(f + 1) * 256])
        dh = (da * gelu_slope(h)).astype(BF)
        dxn2 = dxn2 + nt(dh, up)
    dy = ct.astype(F32) + norm_back(dxn2 * g2, xh2, rs2)
    gattn = dy.astype(BF)
    dmixt = [nt(wo_ref[...], gattn[rows]).astype(BF) for rows in WINDOWS]
    for group, (first, end) in enumerate(GROUPS):
        width = min(C, end * HD) - first * HD
        span = slice(first * HD, first * HD + width)
        parts = [[], [], [], []]
        for w in range(4):
            dp_all = nn(masked[1, w, first * N:end * N, 0:width], dmixt[w][span, :])
            for n in range(first, end):
                dp = dp_all[(n - first) * N:(n - first + 1) * N]
                p = probs[w, n * N:(n + 1) * N, :].astype(F32)
                pd = p * dp
                ds = pd - p * jnp.sum(pd, axis=0, keepdims=True)
                parts[w].append(ds)
                dscores[w, n * N:(n + 1) * N, :] = ds.astype(BF)
            if w % 2:
                for n in range(first, end):
                    dbias[(w // 2) * HEADS + n] = parts[w - 1][n - first] + parts[w][n - first]
        after_group(group)
    return xh1, rs1, xn1, [v[C:2 * C] for v in qkvt], dy, gattn


def all_finish(state, g1, wq, wk, wv, wo_ref, probs, dscores, halfway):
    picks = head_picks()
    xh1, rs1, xn1, keyst, dy, gattn = state
    queries = nn(xn1, wq[...]).astype(BF)
    dmix = nt(gattn, wo_ref[...]).astype(BF)
    dqs, dks, dvs = [[], [], [], []], [[], [], [], []], [[], [], [], []]
    for first, end in GROUPS:
        width = min(C, end * HD) - first * HD
        span = slice(first * HD, first * HD + width)
        for w, rows in enumerate(WINDOWS):
            for n in range(first, end):
                dqs[w].append(nn(keyst[w][n * HD:(n + 1) * HD], dscores[w, n * N:(n + 1) * N, :]))
            dk_all = nn(dscores[w, first * N:end * N, :], queries[rows, span])
            dv_all = nn(probs[w, first * N:end * N, :], dmix[rows, span])
            for store, full in ((dks, dk_all), (dvs, dv_all)):
                total = jnp.zeros((N, width), F32)
                for n in range(first, end):
                    total = total + full[(n - first) * N:(n - first + 1) * N] * picks[n][:, 0:width]
                store[w].append(total)
    halfway()
    dq = jnp.concatenate([(jnp.concatenate(dqs[w], axis=0) * SCALE).astype(BF).T for w in range(4)], axis=0)
    dk = (jnp.concatenate([jnp.concatenate(dks[w], axis=1) for w in range(4)], axis=0) * SCALE).astype(BF)
    dv = jnp.concatenate([jnp.concatenate(dvs[w], axis=1) for w in range(4)], axis=0).astype(BF)
    dxn1 = nt(dq, wq[...]) + nt(dk, wk[...]) + nt(dv, wv[...])
    return (dy + norm_back(dxn1.astype(BF).astype(F32) * g1, xh1, rs1)).astype(BF)


def group_tables(group):
    first, end = GROUPS[group]
    return [a * HEADS + n for a in range(2) for n in range(first, end)]


def fold_bias(group, dbias, join_ref, own_ref, pick_ref, strips, red):
    tables = group_tables(group)
    count = len(tables)
    for k, an in enumerate(tables):
        total = jnp.zeros((PS, LW), F32)
        for j in range(WW):
            lo = (WW - 1 - j) * PS
            total = total + jnp.pad(dbias[an, j * PS:(j + 1) * PS, :], ((0, 0), (lo, LW - N - lo)))
        strips[k, 0:PS, :] = total
    total = jnp.zeros((count * 24, N), F32)
    for qt in range(PS):
        rows = (strips[0:count, qt, :][:, None, :] * pick_ref[...][None]).reshape(count * 24, LW).astype(BF)
        total = total + nn(rows, join_ref[...]) * own_ref[qt:qt + 1, :].astype(F32)
    tails = jnp.zeros((24, 128), F32)
    for k in range(count):
        tail = jnp.concatenate([total[k * 24:(k + 1) * 24, 128:N], jnp.zeros((24, 112), F32)], axis=1)
        tails = tails + (pltpu.roll(tail, 16 * k, 1) if k else tail)
    rows = red.shape[0] * red.shape[1]
    red[...] = jnp.concatenate(
        [total[:, 0:128], tails, jnp.zeros((rows - (count + 1) * 24, 128), F32)], axis=0).astype(BF).reshape(red.shape)


def unpack_fold(group, full, gb_ref):
    tables = group_tables(group)
    count = len(tables)
    rows = full[...].astype(F32).reshape(full.shape[0] * full.shape[1], 128)
    for k, an in enumerate(tables):
        place = slice(an * OFFS, (an + 1) * OFFS)
        gb_ref[place, 0, 0:128] = rows[k * 24:k * 24 + OFFS]
        gb_ref[place, 0, 128:N] = rows[count * 24:count * 24 + OFFS, 16 * k:16 * (k + 1)]


def prepare_weights(wi_ref, wit, wq, wk, wv):
    wit[...] = wi_ref[...].T
    for k, ref in enumerate((wq, wk, wv)):
        ref[...] = wi_ref[:, k * C:(k + 1) * C]


VM = pl.BlockSpec(memory_space=pltpu.VMEM)

MAIN_SCRATCH = [
    pltpu.VMEM((12, 24, N), F32),
    pltpu.VMEM((12, 16, LW), F32),
    pltpu.VMEM((12, N, N), F32),
    pltpu.VMEM((3 * C, C), BF),
    pltpu.VMEM((C, C), BF),
    pltpu.VMEM((C, C), BF),
    pltpu.VMEM((C, C), BF),
    pltpu.VMEM((2, 4, HEADS * N, 128), BF),
    pltpu.VMEM((4, HEADS * N, N), BF),
    pltpu.VMEM((4, HEADS * N, N), BF),
    pltpu.VMEM((4, C, N), BF),
    pltpu.VMEM((12, N, N), F32),
]


PIECE0, PIECE1 = 80, 48
LAT0, LAT1, OWN1, LON1, DIAG1, ROWS = 80, 160, 208, 256, 304, 352
MESH = pl.DeviceIdType.MESH


def piece_consts():
    pack = np.zeros((2, ROWS, N), np.float32)
    place0 = np.zeros((N, LAT1), np.float32)
    place1 = np.zeros((N, ROWS - LAT1), np.float32)
    for p in range(2):
        for h in range(6):
            own = h >= 3
            s = h - 3 if own else h + 3
            for w in range(24):
                e = (w - 6) % 24
                if e < 12:
                    row = (0 if own else LAT0) + (e * 2 + p) * 3 + s % 3
                    place0[e * PS + p * WH + s, row] = 1
                else:
                    e -= 12
                    base = (OWN1 if own else LAT1) if e < 6 else (LON1 if own else DIAG1)
                    row = base + ((e % 6) * 2 + p) * 3 + s % 3
                    place1[e * PS + p * WH + s, row - LAT1] = 1
                pack[p, row, h * 24 + w] = 1
    return pack, place0, place1


def lat_lon():
    return lax.axis_index("lat"), lax.axis_index("lon")


def shifted(lat, lon, da, do):
    return lax.rem(lat + 4 + da, 4), lax.rem(lon + 64 + do, 64)


def halo_copies(plan, box, land, lat, lon, send_sem, recv_sem):
    return [
        pltpu.make_async_remote_copy(
            src_ref=box.at[pl.ds(start, size)],
            dst_ref=land.at[pl.ds(target, size)],
            send_sem=send_sem.at[k],
            recv_sem=recv_sem.at[k],
            device_id=shifted(lat, lon, *step),
            device_id_type=MESH,
        )
        for k, (start, size, target, step) in enumerate(plan)
    ]


IN_PLAN = ((0, 128, LAT0, (-1, 0)), (128, 48, LON1, (0, -1)), (176, 48, DIAG1, (-1, -1)))
BACK_PLAN = ((LAT0, 128, LAT0, (1, 0)), (LON1, 48, LON1, (0, 1)), (DIAG1, 48, DIAG1, (1, 1)))


def deep_peer(lon, d):
    high, z, y = lon // 32, lax.rem(lon // 4, 8), lax.rem(lon, 4)
    return (high * 8 + lax.rem(z + d, 8)) * 4 + y


def plane_place(lon):
    return (lon // 32) * 4 + lax.rem(lon, 4)


def flat_peer(lon, d):
    z = lax.rem(lon // 4, 8)
    place = lax.rem(plane_place(lon) + d, 8)
    return ((place // 4) * 8 + z) * 4 + lax.rem(place, 4)


def sum_copies(kind, lon, lat, src, dst, send_sem, recv_sem):
    place = plane_place(lon)
    copies = []
    for d in (4, 3, 5, 2, 6, 1, 7) if kind == 1 else (6, 2, 5, 7, 4, 1, 3):
        if kind == 0:
            peer, source, target = flat_peer(lon, d), src.at[lax.rem(place + d, 8)], dst.at[d - 1]
        elif kind == 1:
            peer, source, target = deep_peer(lon, d), src, dst.at[d - 1]
        else:
            peer, source, target = flat_peer(lon, d), src, dst.at[place]
        copies.append(pltpu.make_async_remote_copy(
            src_ref=source, dst_ref=target, send_sem=send_sem.at[kind, d - 1], recv_sem=recv_sem.at[kind, d - 1],
            device_id=(lat, peer), device_id_type=MESH))
    return copies


def add_up(own, slots):
    total = own.astype(F32)
    for d in range(7):
        total = total + slots[d].astype(F32)
    return total.astype(BF)


LOCAL = (
    ((4, N, C), BF), ((4, N, C), BF), ((2, ROWS, N), BF), ((N, LAT1), BF), ((N, ROWS - LAT1), BF),
    ((12 * OFFS, 1, N), F32), ((1, C), F32), ((1, C), F32), ((C, 3 * C), BF), ((C, C), BF), ((C, FF), BF), ((C, FF), BF),
    ((LW, N), BF), ((N, LW), BF), ((16, N), BF), ((24, LW), F32), ((2, N, ROWS), BF), ((LAT1, N), BF), ((ROWS - LAT1, N), BF),
)


def block_kernel(*refs):
    count = len(LOCAL)
    far = refs[:count]
    gx_ref, gb_ref = refs[count:count + 2]
    near = refs[count + 2:2 * count + 2]
    (x_ref, ct_ref, pack_ref, place0_ref, place1_ref, tb_ref, g1_ref, g2_ref, wi_ref, wo_ref, wu_ref, wdt_ref,
     join_ref, joint_ref, own_ref, pick_ref, unpack_ref, unplace0_ref, unplace1_ref) = near
    (t24, strips, bias, wit, wq, wk, wv, masked, probs, dscores, mixed, dbias,
     out_box, land, back_box, back_land, *rest) = refs[2 * count + 2:]
    buffers, rest = (rest[0:6], rest[6:12]), rest[12:]
    near_sem, in_send, in_recv, back_send, back_recv, sum_send, sum_recv = rest
    lat, lon = lat_lon()
    mine = plane_place(lon)

    barrier = pltpu.get_barrier_semaphore()
    for da, do in ((1, 0), (0, 1), (1, 1), (-1, 0), (0, -1), (-1, -1)):
        pl.semaphore_signal(barrier, inc=1, device_id=shifted(lat, lon, da, do), device_id_type=MESH)
    fetches = [pltpu.make_async_copy(far[k], near[k], near_sem.at[k]) for k in range(count)]
    for fetch in fetches:
        fetch.start()
    for d in range(1, 8):
        pl.semaphore_signal(barrier, inc=1, device_id=(lat, deep_peer(lon, d)), device_id_type=MESH)
        pl.semaphore_signal(barrier, inc=1, device_id=(lat, flat_peer(lon, d)), device_id_type=MESH)
    for fetch in fetches[0:3]:
        fetch.wait()

    arrivals = []
    for k, ref in enumerate((x_ref, ct_ref)):
        for a in range(2):
            piece = (nn(pack_ref[0], ref[(2 * a + 1) % 4]) + nn(pack_ref[1], ref[(2 * a + 2) % 4])).astype(BF)
            lanes = slice(a * C, (a + 1) * C)
            land[k, 0:LAT0, lanes] = piece[0:LAT0]
            land[k, OWN1:LON1, lanes] = piece[OWN1:LON1]
            out_box[k, 0:128, lanes] = piece[LAT0:OWN1]
            out_box[k, 128:224, lanes] = piece[LON1:ROWS]
        if k == 0:
            pl.semaphore_wait(barrier, 20)
        arrivals.append(halo_copies(IN_PLAN, out_box.at[k], land.at[k], lat, lon, in_send.at[k], in_recv.at[k]))
        for copy in arrivals[k]:
            copy.start()

    for fetch in fetches[3:]:
        fetch.wait()
    t24[...] = jnp.zeros_like(t24)
    for an in range(12):
        t24[an, 0:OFFS, :] = tb_ref[an * OFFS:(an + 1) * OFFS, 0, :]
    prepare_weights(wi_ref, wit, wq, wk, wv)
    expand_bias(lat, joint_ref, own_ref, pick_ref, t24, strips, bias)
    g1, g2 = g1_ref[...], g2_ref[...]

    sums = []
    for g, (red, slots1, part, slots2, whole, full) in enumerate(buffers):
        sums.append([sum_copies(kind, lon, lat, src, dst, sum_send.at[g], sum_recv.at[g])
                     for kind, (src, dst) in enumerate(((red, slots1), (part, slots2), (whole, full)))])

    def sum_first(g):
        fold_bias(g, dbias, join_ref, own_ref, pick_ref, strips, buffers[g][0])
        for copy in sums[g][0]:
            copy.start()

    def sum_second(g):
        red, slots1, part = buffers[g][0:3]
        for copy in sums[g][0]:
            copy.wait_recv()
        part[...] = add_up(red[mine], slots1)
        for copy in sums[g][1]:
            copy.start()

    def sum_third(g):
        part, slots2, whole, full = buffers[g][2:6]
        for copy in sums[g][1]:
            copy.wait_recv()
        whole[...] = add_up(part[...], slots2)
        for copy in sums[g][2]:
            copy.start()
        full[mine] = whole[...]

    def sum_last(g):
        for copy in sums[g][2]:
            copy.wait_recv()
        unpack_fold(g, buffers[g][5], gb_ref)

    def windows(k):
        for copy in arrivals[k]:
            copy.wait()
        first = nn(place0_ref[...], land[k, 0:LAT1, :]).astype(BF)
        second = nn(place1_ref[...], land[k, LAT1:ROWS, :]).astype(BF)
        return jnp.concatenate([v[:, a * C:(a + 1) * C] for a in range(2) for v in (first, second)], axis=0)

    state = all_scores(windows(0), lambda: windows(1), g1, g2, wq, wk, wv, wit, wo_ref, wu_ref, wdt_ref, bias,
                       masked, probs, dscores, mixed, dbias, sum_first)
    gi = all_finish(state, g1, wq, wk, wv, wo_ref, probs, dscores, lambda: sum_second(0))
    for a in range(2):
        lanes = slice(a * C, (a + 1) * C)
        first = nn(unplace0_ref[...], gi[WINDOWS[2 * a]]).astype(BF)
        second = nn(unplace1_ref[...], gi[WINDOWS[2 * a + 1]]).astype(BF)
        back_land[0:LAT0, lanes] = first[0:LAT0]
        back_land[OWN1:LON1, lanes] = second[OWN1 - LAT1:LON1 - LAT1]
        back_box[LAT0:LAT1, lanes] = first[LAT0:LAT1]
        back_box[LAT1:OWN1, lanes] = second[0:OWN1 - LAT1]
        back_box[LON1:ROWS, lanes] = second[LON1 - LAT1:]
    returns = halo_copies(BACK_PLAN, back_box, back_land, lat, lon, back_send, back_recv)
    for copy in returns:
        copy.start()
    sum_second(1)
    sum_third(0)
    sum_third(1)
    for copy in returns:
        copy.wait()
    for a in range(2):
        for p in range(2):
            gx_ref[(2 * a + 1 + p) % 4] = nn(unpack_ref[p], back_land[:, a * C:(a + 1) * C]).astype(BF)
    sum_last(0)
    for chain in sums:
        for phase in chain[0:2]:
            for copy in phase:
                copy.wait_send()
    sum_last(1)
    for chain in sums:
        for copy in chain[2]:
            copy.wait_send()


def sum_buffers(rows):
    return [pltpu.VMEM(lead + (rows, 128), BF) for lead in ((8,), (7,), (), (7,), (), (8,))]


def block_call(*operands):
    anywhere = pl.BlockSpec(memory_space=pl.ANY)
    dma = pltpu.SemaphoreType.DMA
    return pl.pallas_call(
        block_kernel,
        out_shape=(pltpu.VMEM((4, N, C), BF), pltpu.VMEM((12 * OFFS, 1, N), F32)),
        in_specs=[anywhere] * len(LOCAL),
        out_specs=(VM, VM),
        scratch_shapes=[pltpu.VMEM(*one) for one in LOCAL] + MAIN_SCRATCH + [
            pltpu.VMEM((2, 224, 2 * C), BF),
            pltpu.VMEM((2, ROWS, 2 * C), BF),
            pltpu.VMEM((ROWS, 2 * C), BF),
            pltpu.VMEM((ROWS, 2 * C), BF),
        ] + sum_buffers(32) + sum_buffers(16) + [
            dma((len(LOCAL),)), dma((2, 3)), dma((2, 3)), dma((3,)), dma((3,)), dma((2, 3, 7)), dma((2, 3, 7)),
        ],
        compiler_params=pltpu.CompilerParams(collective_id=0, has_side_effects=True, vmem_limit_bytes=60 * 1024 * 1024),
    )(*operands)


def on_device(block_input, cotangent, first_gain, second_gain, input_weight, output_weight, up_weight,
              down_weight, bias_table):
    join, own, pick = fold_consts()
    pack, place0, place1 = piece_consts()
    as_bf = lambda v: jnp.asarray(v, BF)
    gx, gb = block_call(
        block_input.reshape(4, N, C), cotangent.reshape(4, N, C), as_bf(pack), as_bf(place0), as_bf(place1),
        bias_table.reshape(12 * OFFS, 1, N),
        first_gain[None], second_gain[None], input_weight, output_weight, up_weight, down_weight.T,
        as_bf(join), as_bf(join.T), as_bf(own), jnp.asarray(pick), as_bf(pack.transpose(0, 2, 1)), as_bf(place0.T), as_bf(place1.T))
    return gx.reshape(block_input.shape), gb.reshape(bias_table.shape)


def solution(mesh):
    P = jax.sharding.PartitionSpec
    in_specs = (
        P(None, "lat", "lon", None),
        P(None, "lat", "lon", None),
        P(), P(), P(), P(), P(), P(),
        P(None, "lat", None, None, None),
    )
    out_specs = (P(None, "lat", "lon", None), P(None, "lat", None, None, None))
    return jax.shard_map(on_device, mesh=mesh, in_specs=in_specs, out_specs=out_specs, check_vma=False)
```

```python
import functools
import numpy as np
import jax
import jax.numpy as jnp
from jax import lax
from jax.experimental import pallas as pl
from jax.experimental.pallas import tpu as pltpu

BF = jnp.bfloat16
F32 = jnp.float32
HEADS, WZ, WH, WW = 6, 2, 6, 12
HD = 32
C = 192
FF = 768
N = 144
PS = WZ * WH
OFFS = 2 * WW - 1
LW = 384
EPS = 1e-05
SCALE = HD ** -0.5
NEG = -1e30
LOG2E = 1.4426950408889634


def nn(a, b):
    return lax.dot_general(a, b, (((1,), (0,)), ((), ())), preferred_element_type=F32)


def nt(a, b):
    return lax.dot_general(a, b, (((1,), (1,)), ((), ())), preferred_element_type=F32)


def tn(a, b):
    return lax.dot_general(a, b, (((0,), (0,)), ((), ())), preferred_element_type=F32)


def fold_consts():
    join = np.zeros((LW, N), np.float32)
    own = np.zeros((16, N), np.float32)
    for p in range(WZ):
        for q in range(WZ):
            for s in range(WH):
                for t in range(WH):
                    m = ((p * WZ + q) * WH + s) * WH + t
                    own[q * WH + t, m] = 1
                    join[p * WH + s:OFFS * PS:PS, m] = 1
    pick = np.zeros((24, LW), np.float32)
    for r in range(OFFS):
        pick[r, r * PS:(r + 1) * PS] = 1
    return join, own, pick


def normalize(v):
    centred = v - jnp.mean(v, axis=-1, keepdims=True)
    rs = lax.rsqrt(jnp.mean(centred * centred, axis=-1, keepdims=True) + EPS)
    return centred * rs, rs


def norm_back(g, xh, rs):
    return rs * (g - jnp.mean(g, axis=-1, keepdims=True) - xh * jnp.mean(g * xh, axis=-1, keepdims=True))


def gelu_slope(h):
    cdf = 0.5 + 0.5 * lax.erf(h * 0.7071067811865476)
    return cdf + h * (jnp.exp(-0.5 * (h * h)) * 0.3989422804014327)


def expand_bias(lat, joint_ref, own_ref, pick_ref, t24, strips, bias):
    table = t24[...].reshape(12 * 24, N)
    hi = table.astype(BF)
    low = (table - hi.astype(F32)).astype(BF)
    pick = pick_ref[...][None] * LOG2E
    for qt in range(PS):
        own = own_ref[qt:qt + 1, :]
        wide = nn(hi * own, joint_ref[...]) + nn(low * own, joint_ref[...])
        strips[:, qt, :] = jnp.sum(wide.reshape(12, 24, LW) * pick, axis=1)
    row = lax.broadcasted_iota(jnp.int32, (N, N), 0).astype(F32)
    col = lax.broadcasted_iota(jnp.int32, (N, N), 1).astype(F32)

    def place(v):
        ps = v - PS * jnp.floor((v + 0.5) * (1.0 / PS))
        upper = (ps >= WH).astype(F32)
        s = ps - WH * upper
        return upper, (s >= WH // 2).astype(F32)

    rp, rs = place(row)
    cp, cs = place(col)
    last_band = (lat == 3).astype(F32)
    apart_rows = jnp.abs(rs - cs) * last_band
    apart_levels = jnp.abs(rp - cp)
    for a in range(2):
        apart = apart_rows + apart_levels if a else apart_rows
        excluded = jnp.where(apart > 0.5, NEG, 0.0)
        for an in range(a * HEADS, (a + 1) * HEADS):
            strip = strips[an, 0:PS, :]
            for j in range(WW):
                lo = (WW - 1 - j) * PS
                rows = slice(j * PS, (j + 1) * PS)
                bias[an, rows, :] = strip[:, lo:lo + N] + excluded[rows]


GROUPS = ((0, 4), (4, 6))


def head_picks():
    lane = lax.broadcasted_iota(jnp.int32, (1, 128), 1)
    return [((lane >= n * HD % 128) & (lane < n * HD % 128 + HD)).astype(F32) for n in range(HEADS)]


WINDOWS = [slice(w * N, (w + 1) * N) for w in range(4)]


def all_scores(x, late_ct, g1, g2, wq, wk, wv, wqkvt, wo_ref, wu_ref, wdt_ref,
               bias, masked, blocks, probs, dscores, mixed, dbias, after_group):
    picks16 = [v.astype(BF) for v in head_picks()]

    def by_head(w, v, kind):
        for n in range(HEADS):
            if n < 4:
                masked[kind, w, n * N:(n + 1) * N, :] = v[:, 0:128] * picks16[n]
            else:
                masked[kind, w, n * N:(n + 1) * N, 0:64] = v[:, 128:C] * picks16[n][:, 0:64]

    x = x.astype(F32)
    xh1, rs1 = normalize(x)
    xn1 = (xh1 * g1).astype(BF)
    keys = nn(xn1, wk[...]).astype(BF)
    values = nn(xn1, wv[...]).astype(BF)
    qkvt = [nt(wqkvt[...], xn1[rows]).astype(BF) for rows in WINDOWS]
    for w, rows in enumerate(WINDOWS):
        by_head(w, keys[rows], 0)
        by_head(w, values[rows], 1)
        for n in range(HEADS):
            for k in range(2):
                blocks[k, w, n * HD:(n + 1) * HD, n * N:(n + 1) * N] = (
                    qkvt[w][(2 - k) * C + n * HD:(2 - k) * C + (n + 1) * HD])
    for first, end in GROUPS:
        width = min(C, end * HD) - first * HD
        for w in range(4):
            s_all = nn(masked[0, w, first * N:end * N, 0:width], qkvt[w][first * HD:end * HD, :])
            for n in range(first, end):
                s = s_all[(n - first) * N:(n - first + 1) * N] * (SCALE * LOG2E) + bias[(w // 2) * HEADS + n]
                e = jnp.exp2(s - jnp.max(s, axis=0, keepdims=True))
                p = (e * (1.0 / jnp.sum(e, axis=0, keepdims=True))).astype(BF)
                probs[w, n * N:(n + 1) * N, :] = p
    for w in range(4):
        mixed[w] = nn(blocks[0, w], probs[w]).astype(BF)
    ct = late_ct()
    attn = jnp.concatenate([tn(mixed[w], wo_ref[...]) for w in range(4)], axis=0).astype(BF)
    y = x + attn.astype(F32)
    xh2, rs2 = normalize(y)
    xn2 = (xh2 * g2).astype(BF)
    dxn2 = jnp.zeros((4 * N, C), F32)
    for f in range(FF // 256):
        up = wu_ref[:, f * 256:(f + 1) * 256]
        h = nn(xn2, up)
        da = nn(ct, wdt_ref[:, f * 256:(f + 1) * 256])
        dh = (da * gelu_slope(h)).astype(BF)
        dxn2 = dxn2 + nt(dh, up)
    dy = ct.astype(F32) + norm_back(dxn2 * g2, xh2, rs2)
    gattn = dy.astype(BF)
    dmixt = [nt(wo_ref[...], gattn[rows]).astype(BF) for rows in WINDOWS]
    for group, (first, end) in enumerate(GROUPS):
        width = min(C, end * HD) - first * HD
        span = slice(first * HD, first * HD + width)
        parts = [[], [], [], []]
        for w in range(4):
            dp_all = nn(masked[1, w, first * N:end * N, 0:width], dmixt[w][span, :])
            for n in range(first, end):
                dp = dp_all[(n - first) * N:(n - first + 1) * N]
                p = probs[w, n * N:(n + 1) * N, :].astype(F32)
                pd = p * dp
                ds = pd - p * jnp.sum(pd, axis=0, keepdims=True)
                parts[w].append(ds)
                dscores[w, n * N:(n + 1) * N, :] = ds.astype(BF)
            if w % 2:
                for n in range(first, end):
                    dbias[(w // 2) * HEADS + n] = parts[w - 1][n - first] + parts[w][n - first]
        after_group(group)
    return xh1, rs1, xn1, dy, gattn


def all_finish(state, g1, wq, wk, wv, wo_ref, blocks, probs, dscores, halfway):
    picks = head_picks()
    xh1, rs1, xn1, dy, gattn = state
    queries = nn(xn1, wq[...]).astype(BF)
    dmix = nt(gattn, wo_ref[...]).astype(BF)
    dqs = [nn(blocks[1, w], dscores[w]) for w in range(4)]
    dks, dvs = [[], [], [], []], [[], [], [], []]
    for first, end in GROUPS:
        width = min(C, end * HD) - first * HD
        span = slice(first * HD, first * HD + width)
        for w, rows in enumerate(WINDOWS):
            dk_all = nn(dscores[w, first * N:end * N, :], queries[rows, span])
            dv_all = nn(probs[w, first * N:end * N, :], dmix[rows, span])
            for store, full in ((dks, dk_all), (dvs, dv_all)):
                total = jnp.zeros((N, width), F32)
                for n in range(first, end):
                    total = total + full[(n - first) * N:(n - first + 1) * N] * picks[n][:, 0:width]
                store[w].append(total)
    halfway()
    dq = jnp.concatenate([(dqs[w] * SCALE).astype(BF).T for w in range(4)], axis=0)
    dk = (jnp.concatenate([jnp.concatenate(dks[w], axis=1) for w in range(4)], axis=0) * SCALE).astype(BF)
    dv = jnp.concatenate([jnp.concatenate(dvs[w], axis=1) for w in range(4)], axis=0).astype(BF)
    dxn1 = nt(dq, wq[...]) + nt(dk, wk[...]) + nt(dv, wv[...])
    return (dy + norm_back(dxn1.astype(BF).astype(F32) * g1, xh1, rs1)).astype(BF)


def group_tables(group):
    first, end = GROUPS[group]
    return [a * HEADS + n for a in range(2) for n in range(first, end)]


def fold_bias(group, dbias, join_ref, own_ref, pick_ref, strips, red):
    tables = group_tables(group)
    count = len(tables)
    for k, an in enumerate(tables):
        total = jnp.zeros((PS, LW), F32)
        for j in range(WW):
            lo = (WW - 1 - j) * PS
            total = total + jnp.pad(dbias[an, j * PS:(j + 1) * PS, :], ((0, 0), (lo, LW - N - lo)))
        strips[k, 0:PS, :] = total
    total = jnp.zeros((count * 24, N), F32)
    for qt in range(PS):
        rows = (strips[0:count, qt, :][:, None, :] * pick_ref[...][None]).reshape(count * 24, LW).astype(BF)
        total = total + nn(rows, join_ref[...]) * own_ref[qt:qt + 1, :].astype(F32)
    tails = jnp.zeros((24, 128), F32)
    for k in range(count):
        tail = jnp.concatenate([total[k * 24:(k + 1) * 24, 128:N], jnp.zeros((24, 112), F32)], axis=1)
        tails = tails + (pltpu.roll(tail, 16 * k, 1) if k else tail)
    rows = red.shape[0] * red.shape[1]
    red[...] = jnp.concatenate(
        [total[:, 0:128], tails, jnp.zeros((rows - (count + 1) * 24, 128), F32)], axis=0).astype(BF).reshape(red.shape)


def unpack_fold(group, full, gb_ref):
    tables = group_tables(group)
    count = len(tables)
    rows = full[...].astype(F32).reshape(full.shape[0] * full.shape[1], 128)
    for k, an in enumerate(tables):
        place = slice(an * OFFS, (an + 1) * OFFS)
        gb_ref[place, 0, 0:128] = rows[k * 24:k * 24 + OFFS]
        gb_ref[place, 0, 128:N] = rows[count * 24:count * 24 + OFFS, 16 * k:16 * (k + 1)]


def prepare_weights(wi_ref, wit, wq, wk, wv):
    wit[...] = wi_ref[...].T
    for k, ref in enumerate((wq, wk, wv)):
        ref[...] = wi_ref[:, k * C:(k + 1) * C]


VM = pl.BlockSpec(memory_space=pltpu.VMEM)

MAIN_SCRATCH = [
    pltpu.VMEM((12, 24, N), F32),
    pltpu.VMEM((12, 16, LW), F32),
    pltpu.VMEM((12, N, N), F32),
    pltpu.VMEM((3 * C, C), BF),
    pltpu.VMEM((C, C), BF),
    pltpu.VMEM((C, C), BF),
    pltpu.VMEM((C, C), BF),
    pltpu.VMEM((2, 4, HEADS * N, 128), BF),
    pltpu.VMEM((2, 4, C, HEADS * N), BF),
    pltpu.VMEM((4, HEADS * N, N), BF),
    pltpu.VMEM((4, HEADS * N, N), BF),
    pltpu.VMEM((4, C, N), BF),
    pltpu.VMEM((12, N, N), F32),
]


PIECE0, PIECE1 = 80, 48
LAT0, LAT1, OWN1, LON1, DIAG1, ROWS = 80, 160, 208, 256, 304, 352
MESH = pl.DeviceIdType.MESH


def piece_consts():
    pack = np.zeros((2, ROWS, N), np.float32)
    place0 = np.zeros((N, LAT1), np.float32)
    place1 = np.zeros((N, ROWS - LAT1), np.float32)
    for p in range(2):
        for h in range(6):
            own = h >= 3
            s = h - 3 if own else h + 3
            for w in range(24):
                e = (w - 6) % 24
                if e < 12:
                    row = (0 if own else LAT0) + (e * 2 + p) * 3 + s % 3
                    place0[e * PS + p * WH + s, row] = 1
                else:
                    e -= 12
                    base = (OWN1 if own else LAT1) if e < 6 else (LON1 if own else DIAG1)
                    row = base + ((e % 6) * 2 + p) * 3 + s % 3
                    place1[e * PS + p * WH + s, row - LAT1] = 1
                pack[p, row, h * 24 + w] = 1
    return pack, place0, place1


def lat_lon():
    return lax.axis_index("lat"), lax.axis_index("lon")


def shifted(lat, lon, da, do):
    return lax.rem(lat + 4 + da, 4), lax.rem(lon + 64 + do, 64)


def halo_copies(plan, box, land, lat, lon, send_sem, recv_sem):
    return [
        pltpu.make_async_remote_copy(
            src_ref=box.at[pl.ds(start, size)],
            dst_ref=land.at[pl.ds(target, size)],
            send_sem=send_sem.at[k],
            recv_sem=recv_sem.at[k],
            device_id=shifted(lat, lon, *step),
            device_id_type=MESH,
        )
        for k, (start, size, target, step) in enumerate(plan)
    ]


IN_PLAN = ((0, 128, LAT0, (-1, 0)), (128, 48, LON1, (0, -1)), (176, 48, DIAG1, (-1, -1)))
BACK_PLAN = ((LAT0, 128, LAT0, (1, 0)), (LON1, 48, LON1, (0, 1)), (DIAG1, 48, DIAG1, (1, 1)))


def deep_peer(lon, d):
    high, z, y = lon // 32, lax.rem(lon // 4, 8), lax.rem(lon, 4)
    return (high * 8 + lax.rem(z + d, 8)) * 4 + y


def plane_place(lon):
    return (lon // 32) * 4 + lax.rem(lon, 4)


def flat_peer(lon, d):
    z = lax.rem(lon // 4, 8)
    place = lax.rem(plane_place(lon) + d, 8)
    return ((place // 4) * 8 + z) * 4 + lax.rem(place, 4)


def sum_copies(kind, lon, lat, src, dst, send_sem, recv_sem):
    place = plane_place(lon)
    copies = []
    for d in (4, 3, 5, 2, 6, 1, 7) if kind == 1 else (6, 2, 5, 7, 4, 1, 3):
        if kind == 0:
            peer, source, target = flat_peer(lon, d), src.at[lax.rem(place + d, 8)], dst.at[d - 1]
        elif kind == 1:
            peer, source, target = deep_peer(lon, d), src, dst.at[d - 1]
        else:
            peer, source, target = flat_peer(lon, d), src, dst.at[place]
        copies.append(pltpu.make_async_remote_copy(
            src_ref=source, dst_ref=target, send_sem=send_sem.at[kind, d - 1], recv_sem=recv_sem.at[kind, d - 1],
            device_id=(lat, peer), device_id_type=MESH))
    return copies


def add_up(own, slots):
    total = own.astype(F32)
    for d in range(7):
        total = total + slots[d].astype(F32)
    return total.astype(BF)


LOCAL = (
    ((4, N, C), BF), ((4, N, C), BF), ((2, ROWS, N), BF), ((N, LAT1), BF), ((N, ROWS - LAT1), BF),
    ((12 * OFFS, 1, N), F32), ((1, C), F32), ((1, C), F32), ((C, 3 * C), BF), ((C, C), BF), ((C, FF), BF), ((C, FF), BF),
    ((LW, N), BF), ((N, LW), BF), ((16, N), BF), ((24, LW), F32), ((2, N, ROWS), BF), ((LAT1, N), BF), ((ROWS - LAT1, N), BF),
)


def block_kernel(*refs):
    count = len(LOCAL)
    far = refs[:count]
    gx_ref, gb_ref = refs[count:count + 2]
    near = refs[count + 2:2 * count + 2]
    (x_ref, ct_ref, pack_ref, place0_ref, place1_ref, tb_ref, g1_ref, g2_ref, wi_ref, wo_ref, wu_ref, wdt_ref,
     join_ref, joint_ref, own_ref, pick_ref, unpack_ref, unplace0_ref, unplace1_ref) = near
    (t24, strips, bias, wit, wq, wk, wv, masked, blocks, probs, dscores, mixed, dbias,
     out_box, land, back_box, back_land, *rest) = refs[2 * count + 2:]
    buffers, rest = (rest[0:6], rest[6:12]), rest[12:]
    near_sem, in_send, in_recv, back_send, back_recv, sum_send, sum_recv = rest
    lat, lon = lat_lon()
    mine = plane_place(lon)

    barrier = pltpu.get_barrier_semaphore()
    for da, do in ((1, 0), (0, 1), (1, 1), (-1, 0), (0, -1), (-1, -1)):
        pl.semaphore_signal(barrier, inc=1, device_id=shifted(lat, lon, da, do), device_id_type=MESH)
    fetches = [pltpu.make_async_copy(far[k], near[k], near_sem.at[k]) for k in range(count)]
    for fetch in fetches:
        fetch.start()
    for d in range(1, 8):
        pl.semaphore_signal(barrier, inc=1, device_id=(lat, deep_peer(lon, d)), device_id_type=MESH)
        pl.semaphore_signal(barrier, inc=1, device_id=(lat, flat_peer(lon, d)), device_id_type=MESH)
    for fetch in fetches[0:3]:
        fetch.wait()

    arrivals = []
    for k, ref in enumerate((x_ref, ct_ref)):
        for a in range(2):
            piece = (nn(pack_ref[0], ref[(2 * a + 1) % 4]) + nn(pack_ref[1], ref[(2 * a + 2) % 4])).astype(BF)
            lanes = slice(a * C, (a + 1) * C)
            land[k, 0:LAT0, lanes] = piece[0:LAT0]
            land[k, OWN1:LON1, lanes] = piece[OWN1:LON1]
            out_box[k, 0:128, lanes] = piece[LAT0:OWN1]
            out_box[k, 128:224, lanes] = piece[LON1:ROWS]
        if k == 0:
            pl.semaphore_wait(barrier, 20)
        arrivals.append(halo_copies(IN_PLAN, out_box.at[k], land.at[k], lat, lon, in_send.at[k], in_recv.at[k]))
        for copy in arrivals[k]:
            copy.start()

    for fetch in fetches[3:]:
        fetch.wait()
    t24[...] = jnp.zeros_like(t24)
    blocks[...] = jnp.zeros_like(blocks)
    for an in range(12):
        t24[an, 0:OFFS, :] = tb_ref[an * OFFS:(an + 1) * OFFS, 0, :]
    prepare_weights(wi_ref, wit, wq, wk, wv)
    expand_bias(lat, joint_ref, own_ref, pick_ref, t24, strips, bias)
    g1, g2 = g1_ref[...], g2_ref[...]

    sums = []
    for g, (red, slots1, part, slots2, whole, full) in enumerate(buffers):
        sums.append([sum_copies(kind, lon, lat, src, dst, sum_send.at[g], sum_recv.at[g])
                     for kind, (src, dst) in enumerate(((red, slots1), (part, slots2), (whole, full)))])

    def sum_first(g):
        fold_bias(g, dbias, join_ref, own_ref, pick_ref, strips, buffers[g][0])
        for copy in sums[g][0]:
            copy.start()

    def sum_second(g):
        red, slots1, part = buffers[g][0:3]
        for copy in sums[g][0]:
            copy.wait_recv()
        part[...] = add_up(red[mine], slots1)
        for copy in sums[g][1]:
            copy.start()

    def sum_third(g):
        part, slots2, whole, full = buffers[g][2:6]
        for copy in sums[g][1]:
            copy.wait_recv()
        whole[...] = add_up(part[...], slots2)
        for copy in sums[g][2]:
            copy.start()
        full[mine] = whole[...]

    def sum_last(g):
        for copy in sums[g][2]:
            copy.wait_recv()
        unpack_fold(g, buffers[g][5], gb_ref)

    def windows(k):
        for copy in arrivals[k]:
            copy.wait()
        first = nn(place0_ref[...], land[k, 0:LAT1, :]).astype(BF)
        second = nn(place1_ref[...], land[k, LAT1:ROWS, :]).astype(BF)
        return jnp.concatenate([v[:, a * C:(a + 1) * C] for a in range(2) for v in (first, second)], axis=0)

    state = all_scores(windows(0), lambda: windows(1), g1, g2, wq, wk, wv, wit, wo_ref, wu_ref, wdt_ref, bias,
                       masked, blocks, probs, dscores, mixed, dbias, sum_first)
    gi = all_finish(state, g1, wq, wk, wv, wo_ref, blocks, probs, dscores, lambda: sum_second(0))
    for a in range(2):
        lanes = slice(a * C, (a + 1) * C)
        first = nn(unplace0_ref[...], gi[WINDOWS[2 * a]]).astype(BF)
        second = nn(unplace1_ref[...], gi[WINDOWS[2 * a + 1]]).astype(BF)
        back_land[0:LAT0, lanes] = first[0:LAT0]
        back_land[OWN1:LON1, lanes] = second[OWN1 - LAT1:LON1 - LAT1]
        back_box[LAT0:LAT1, lanes] = first[LAT0:LAT1]
        back_box[LAT1:OWN1, lanes] = second[0:OWN1 - LAT1]
        back_box[LON1:ROWS, lanes] = second[LON1 - LAT1:]
    returns = halo_copies(BACK_PLAN, back_box, back_land, lat, lon, back_send, back_recv)
    for copy in returns:
        copy.start()
    sum_second(1)
    sum_third(0)
    sum_third(1)
    for copy in returns:
        copy.wait()
    for a in range(2):
        for p in range(2):
            gx_ref[(2 * a + 1 + p) % 4] = nn(unpack_ref[p], back_land[:, a * C:(a + 1) * C]).astype(BF)
    sum_last(0)
    for chain in sums:
        for phase in chain[0:2]:
            for copy in phase:
                copy.wait_send()
    sum_last(1)
    for chain in sums:
        for copy in chain[2]:
            copy.wait_send()


def sum_buffers(rows):
    return [pltpu.VMEM(lead + (rows, 128), BF) for lead in ((8,), (7,), (), (7,), (), (8,))]


def block_call(*operands):
    anywhere = pl.BlockSpec(memory_space=pl.ANY)
    dma = pltpu.SemaphoreType.DMA
    return pl.pallas_call(
        block_kernel,
        out_shape=(pltpu.VMEM((4, N, C), BF), pltpu.VMEM((12 * OFFS, 1, N), F32)),
        in_specs=[anywhere] * len(LOCAL),
        out_specs=(VM, VM),
        scratch_shapes=[pltpu.VMEM(*one) for one in LOCAL] + MAIN_SCRATCH + [
            pltpu.VMEM((2, 224, 2 * C), BF),
            pltpu.VMEM((2, ROWS, 2 * C), BF),
            pltpu.VMEM((ROWS, 2 * C), BF),
            pltpu.VMEM((ROWS, 2 * C), BF),
        ] + sum_buffers(32) + sum_buffers(16) + [
            dma((len(LOCAL),)), dma((2, 3)), dma((2, 3)), dma((3,)), dma((3,)), dma((2, 3, 7)), dma((2, 3, 7)),
        ],
        compiler_params=pltpu.CompilerParams(collective_id=0, has_side_effects=True, vmem_limit_bytes=60 * 1024 * 1024),
    )(*operands)


def on_device(block_input, cotangent, first_gain, second_gain, input_weight, output_weight, up_weight,
              down_weight, bias_table):
    join, own, pick = fold_consts()
    pack, place0, place1 = piece_consts()
    as_bf = lambda v: jnp.asarray(v, BF)
    gx, gb = block_call(
        block_input.reshape(4, N, C), cotangent.reshape(4, N, C), as_bf(pack), as_bf(place0), as_bf(place1),
        bias_table.reshape(12 * OFFS, 1, N),
        first_gain[None], second_gain[None], input_weight, output_weight, up_weight, down_weight.T,
        as_bf(join), as_bf(join.T), as_bf(own), jnp.asarray(pick), as_bf(pack.transpose(0, 2, 1)), as_bf(place0.T), as_bf(place1.T))
    return gx.reshape(block_input.shape), gb.reshape(bias_table.shape)


def solution(mesh):
    P = jax.sharding.PartitionSpec
    in_specs = (
        P(None, "lat", "lon", None),
        P(None, "lat", "lon", None),
        P(), P(), P(), P(), P(), P(),
        P(None, "lat", None, None, None),
    )
    out_specs = (P(None, "lat", "lon", None), P(None, "lat", None, None, None))
    return jax.shard_map(on_device, mesh=mesh, in_specs=in_specs, out_specs=out_specs, check_vma=False)
```

```python
import functools
import numpy as np
import jax
import jax.numpy as jnp
from jax import lax
from jax.experimental import pallas as pl
from jax.experimental.pallas import tpu as pltpu

BF = jnp.bfloat16
F32 = jnp.float32
HEADS, WZ, WH, WW = 6, 2, 6, 12
HD = 32
C = 192
FF = 768
N = 144
PS = WZ * WH
OFFS = 2 * WW - 1
LW = 384
EPS = 1e-05
SCALE = HD ** -0.5
NEG = -1e30
LOG2E = 1.4426950408889634


def nn(a, b):
    return lax.dot_general(a, b, (((1,), (0,)), ((), ())), preferred_element_type=F32)


def nt(a, b):
    return lax.dot_general(a, b, (((1,), (1,)), ((), ())), preferred_element_type=F32)


def tn(a, b):
    return lax.dot_general(a, b, (((0,), (0,)), ((), ())), preferred_element_type=F32)


def fold_consts():
    join = np.zeros((LW, N), np.float32)
    own = np.zeros((16, N), np.float32)
    for p in range(WZ):
        for q in range(WZ):
            for s in range(WH):
                for t in range(WH):
                    m = ((p * WZ + q) * WH + s) * WH + t
                    own[q * WH + t, m] = 1
                    join[p * WH + s:OFFS * PS:PS, m] = 1
    pick = np.zeros((24, LW), np.float32)
    for r in range(OFFS):
        pick[r, r * PS:(r + 1) * PS] = 1
    return join, own, pick


def normalize(v):
    centred = v - jnp.mean(v, axis=-1, keepdims=True)
    rs = lax.rsqrt(jnp.mean(centred * centred, axis=-1, keepdims=True) + EPS)
    return centred * rs, rs


def norm_back(g, xh, rs):
    return rs * (g - jnp.mean(g, axis=-1, keepdims=True) - xh * jnp.mean(g * xh, axis=-1, keepdims=True))


def gelu_slope(h):
    cdf = 0.5 + 0.5 * lax.erf(h * 0.7071067811865476)
    return cdf + h * (jnp.exp(-0.5 * (h * h)) * 0.3989422804014327)


def expand_bias(lat, joint_ref, own_ref, pick_ref, t24, strips, bias):
    table = t24[...].reshape(12 * 24, N)
    hi = table.astype(BF)
    low = (table - hi.astype(F32)).astype(BF)
    pick = pick_ref[...][None] * LOG2E
    for qt in range(PS):
        own = own_ref[qt:qt + 1, :]
        wide = nn(hi * own, joint_ref[...]) + nn(low * own, joint_ref[...])
        strips[:, qt, :] = jnp.sum(wide.reshape(12, 24, LW) * pick, axis=1)
    row = lax.broadcasted_iota(jnp.int32, (N, N), 0).astype(F32)
    col = lax.broadcasted_iota(jnp.int32, (N, N), 1).astype(F32)

    def place(v):
        ps = v - PS * jnp.floor((v + 0.5) * (1.0 / PS))
        upper = (ps >= WH).astype(F32)
        s = ps - WH * upper
        return upper, (s >= WH // 2).astype(F32)

    rp, rs = place(row)
    cp, cs = place(col)
    last_band = (lat == 3).astype(F32)
    apart_rows = jnp.abs(rs - cs) * last_band
    apart_levels = jnp.abs(rp - cp)
    for a in range(2):
        apart = apart_rows + apart_levels if a else apart_rows
        excluded = jnp.where(apart > 0.5, NEG, 0.0)
        for an in range(a * HEADS, (a + 1) * HEADS):
            strip = strips[an, 0:PS, :]
            for j in range(WW):
                lo = (WW - 1 - j) * PS
                rows = slice(j * PS, (j + 1) * PS)
                bias[an, rows, :] = strip[:, lo:lo + N] + excluded[rows]


GROUPS = ((0, 4), (4, 6))


def head_picks():
    lane = lax.broadcasted_iota(jnp.int32, (1, 128), 1)
    return [((lane >= n * HD % 128) & (lane < n * HD % 128 + HD)).astype(F32) for n in range(HEADS)]


WINDOWS = [slice(w * N, (w + 1) * N) for w in range(4)]


def all_scores(x, late_ct, g1, g2, wq, wk, wv, wqkvt, wo_ref, wu_ref, wdt_ref,
               bias, masked, blocks, probs, dscores, mixed, dbias, after_group):
    picks16 = [v.astype(BF) for v in head_picks()]

    def by_head(w, v, kind):
        for n in range(HEADS):
            if n < 4:
                masked[kind, w, n * N:(n + 1) * N, :] = v[:, 0:128] * picks16[n]
            else:
                masked[kind, w, n * N:(n + 1) * N, 0:64] = v[:, 128:C] * picks16[n][:, 0:64]

    x = x.astype(F32)
    xh1, rs1 = normalize(x)
    xn1 = (xh1 * g1).astype(BF)
    keys = nn(xn1, wk[...]).astype(BF)
    values = nn(xn1, wv[...]).astype(BF)
    qkvt = [nt(wqkvt[...], xn1[rows]).astype(BF) for rows in WINDOWS]
    for w, rows in enumerate(WINDOWS):
        by_head(w, keys[rows], 0)
        by_head(w, values[rows], 1)
        for n in range(HEADS):
            for k in range(2):
                blocks[k, w, n * HD:(n + 1) * HD, n * N:(n + 1) * N] = (
                    qkvt[w][(2 - k) * C + n * HD:(2 - k) * C + (n + 1) * HD])
    for first, end in GROUPS:
        width = min(C, end * HD) - first * HD
        for w in range(4):
            s_all = nn(masked[0, w, first * N:end * N, 0:width], qkvt[w][first * HD:end * HD, :])
            for n in range(first, end):
                s = s_all[(n - first) * N:(n - first + 1) * N] * (SCALE * LOG2E) + bias[(w // 2) * HEADS + n]
                e = jnp.exp2(s - jnp.max(s, axis=0, keepdims=True))
                p = (e * (1.0 / jnp.sum(e, axis=0, keepdims=True))).astype(BF)
                probs[w, n * N:(n + 1) * N, :] = p
    for w in range(4):
        mixed[w] = nn(blocks[0, w], probs[w]).astype(BF)
    ct = late_ct()
    attn = jnp.concatenate([tn(mixed[w], wo_ref[...]) for w in range(4)], axis=0).astype(BF)
    y = x + attn.astype(F32)
    xh2, rs2 = normalize(y)
    xn2 = (xh2 * g2).astype(BF)
    dxn2 = jnp.zeros((4 * N, C), F32)
    for f in range(FF // 256):
        up = wu_ref[:, f * 256:(f + 1) * 256]
        h = nn(xn2, up)
        da = nn(ct, wdt_ref[:, f * 256:(f + 1) * 256])
        dh = (da * gelu_slope(h)).astype(BF)
        dxn2 = dxn2 + nt(dh, up)
    dy = ct.astype(F32) + norm_back(dxn2 * g2, xh2, rs2)
    gattn = dy.astype(BF)
    dmixt = [nt(wo_ref[...], gattn[rows]).astype(BF) for rows in WINDOWS]
    for group, (first, end) in enumerate(GROUPS):
        width = min(C, end * HD) - first * HD
        span = slice(first * HD, first * HD + width)
        parts = [[], [], [], []]
        for w in range(4):
            dp_all = nn(masked[1, w, first * N:end * N, 0:width], dmixt[w][span, :])
            for n in range(first, end):
                dp = dp_all[(n - first) * N:(n - first + 1) * N]
                p = probs[w, n * N:(n + 1) * N, :].astype(F32)
                pd = p * dp
                ds = pd - p * jnp.sum(pd, axis=0, keepdims=True)
                parts[w].append(ds)
                dscores[w, n * N:(n + 1) * N, :] = ds.astype(BF)
            if w % 2:
                for n in range(first, end):
                    dbias[(w // 2) * HEADS + n] = parts[w - 1][n - first] + parts[w][n - first]
        after_group(group)
    return xh1, rs1, xn1, dy, gattn


def all_finish(state, g1, wq, wk, wv, wo_ref, blocks, probs, dscores, halfway):
    picks = head_picks()
    xh1, rs1, xn1, dy, gattn = state
    queries = nn(xn1, wq[...]).astype(BF)
    dmix = nt(gattn, wo_ref[...]).astype(BF)
    dqs = [nn(blocks[1, w], dscores[w]) for w in range(4)]
    dks, dvs = [[], [], [], []], [[], [], [], []]
    for first, end in GROUPS:
        width = min(C, end * HD) - first * HD
        span = slice(first * HD, first * HD + width)
        for w, rows in enumerate(WINDOWS):
            dk_all = nn(dscores[w, first * N:end * N, :], queries[rows, span])
            dv_all = nn(probs[w, first * N:end * N, :], dmix[rows, span])
            for store, full in ((dks, dk_all), (dvs, dv_all)):
                total = jnp.zeros((N, width), F32)
                for n in range(first, end):
                    total = total + full[(n - first) * N:(n - first + 1) * N] * picks[n][:, 0:width]
                store[w].append(total)
    halfway()
    dq = jnp.concatenate([(dqs[w] * SCALE).astype(BF).T for w in range(4)], axis=0)
    dk = (jnp.concatenate([jnp.concatenate(dks[w], axis=1) for w in range(4)], axis=0) * SCALE).astype(BF)
    dv = jnp.concatenate([jnp.concatenate(dvs[w], axis=1) for w in range(4)], axis=0).astype(BF)
    dxn1 = nt(dq, wq[...]) + nt(dk, wk[...]) + nt(dv, wv[...])
    return (dy + norm_back(dxn1.astype(BF).astype(F32) * g1, xh1, rs1)).astype(BF)


def group_tables(group):
    first, end = GROUPS[group]
    return [a * HEADS + n for a in range(2) for n in range(first, end)]


def diagonals(an, dbias):
    total = jnp.zeros((PS, LW), F32)
    for j in range(WW):
        lo = (WW - 1 - j) * PS
        total = total + jnp.pad(dbias[an, j * PS:(j + 1) * PS, :], ((0, 0), (lo, LW - N - lo)))
    return total


def to_columns(count, rows_of, join_ref, own_ref, pick_ref):
    total = jnp.zeros((count * 24, N), F32)
    for qt in range(PS):
        rows = (rows_of(qt)[:, None, :] * pick_ref[...][None]).reshape(count * 24, LW).astype(BF)
        total = total + nn(rows, join_ref[...]) * own_ref[qt:qt + 1, :].astype(F32)
    return total


def fold_bias(group, dbias, join_ref, own_ref, pick_ref, strips, red):
    tables = group_tables(group)
    count = len(tables)
    if group == 0:
        for k, an in enumerate(tables):
            red[k] = jnp.concatenate([diagonals(an, dbias), jnp.zeros((16 - PS, LW), F32)], axis=0).astype(BF)
        return
    for k, an in enumerate(tables):
        strips[k, 0:PS, :] = diagonals(an, dbias)
    total = to_columns(count, lambda qt: strips[0:count, qt, :], join_ref, own_ref, pick_ref)
    tails = jnp.zeros((24, 128), F32)
    for k in range(count):
        tail = jnp.concatenate([total[k * 24:(k + 1) * 24, 128:N], jnp.zeros((24, 112), F32)], axis=1)
        tails = tails + (pltpu.roll(tail, 16 * k, 1) if k else tail)
    rows = red.shape[0] * red.shape[1]
    red[...] = jnp.concatenate(
        [total[:, 0:128], tails, jnp.zeros((rows - (count + 1) * 24, 128), F32)], axis=0).astype(BF).reshape(red.shape)


def fold_one(strip, join_ref, own_ref, pick_ref):
    total = to_columns(1, lambda qt: strip[qt:qt + 1], join_ref, own_ref, pick_ref)
    tails = jnp.zeros((8, 128), F32)
    for g in range(3):
        tail = jnp.concatenate([total[8 * g:8 * g + 8, 128:N], jnp.zeros((8, 112), F32)], axis=1)
        tails = tails + (pltpu.roll(tail, 16 * g, 1) if g else tail)
    return jnp.concatenate([total[:, 0:128], tails], axis=0).astype(BF)


def unpack_fold(group, full, gb_ref):
    tables = group_tables(group)
    count = len(tables)
    if group == 0:
        for k, an in enumerate(tables):
            rows = full[k].astype(F32)
            gb_ref[an * OFFS:(an + 1) * OFFS, 0, 0:128] = rows[0:OFFS]
            for g in range(3):
                size = min(8, OFFS - 8 * g)
                place = slice(an * OFFS + 8 * g, an * OFFS + 8 * g + size)
                gb_ref[place, 0, 128:N] = rows[24:24 + size, 16 * g:16 * (g + 1)]
        return
    rows = full[...].astype(F32).reshape(full.shape[0] * full.shape[1], 128)
    for k, an in enumerate(tables):
        place = slice(an * OFFS, (an + 1) * OFFS)
        gb_ref[place, 0, 0:128] = rows[k * 24:k * 24 + OFFS]
        gb_ref[place, 0, 128:N] = rows[count * 24:count * 24 + OFFS, 16 * k:16 * (k + 1)]


def prepare_weights(wi_ref, wit, wq, wk, wv):
    wit[...] = wi_ref[...].T
    for k, ref in enumerate((wq, wk, wv)):
        ref[...] = wi_ref[:, k * C:(k + 1) * C]


VM = pl.BlockSpec(memory_space=pltpu.VMEM)

MAIN_SCRATCH = [
    pltpu.VMEM((12, 24, N), F32),
    pltpu.VMEM((12, 16, LW), F32),
    pltpu.VMEM((12, N, N), F32),
    pltpu.VMEM((3 * C, C), BF),
    pltpu.VMEM((C, C), BF),
    pltpu.VMEM((C, C), BF),
    pltpu.VMEM((C, C), BF),
    pltpu.VMEM((2, 4, HEADS * N, 128), BF),
    pltpu.VMEM((2, 4, C, HEADS * N), BF),
    pltpu.VMEM((4, HEADS * N, N), BF),
    pltpu.VMEM((4, HEADS * N, N), BF),
    pltpu.VMEM((4, C, N), BF),
    pltpu.VMEM((12, N, N), F32),
]


PIECE0, PIECE1 = 80, 48
LAT0, LAT1, OWN1, LON1, DIAG1, ROWS = 80, 160, 208, 256, 304, 352
MESH = pl.DeviceIdType.MESH


def piece_consts():
    pack = np.zeros((2, ROWS, N), np.float32)
    place0 = np.zeros((N, LAT1), np.float32)
    place1 = np.zeros((N, ROWS - LAT1), np.float32)
    for p in range(2):
        for h in range(6):
            own = h >= 3
            s = h - 3 if own else h + 3
            for w in range(24):
                e = (w - 6) % 24
                if e < 12:
                    row = (0 if own else LAT0) + (e * 2 + p) * 3 + s % 3
                    place0[e * PS + p * WH + s, row] = 1
                else:
                    e -= 12
                    base = (OWN1 if own else LAT1) if e < 6 else (LON1 if own else DIAG1)
                    row = base + ((e % 6) * 2 + p) * 3 + s % 3
                    place1[e * PS + p * WH + s, row - LAT1] = 1
                pack[p, row, h * 24 + w] = 1
    return pack, place0, place1


def lat_lon():
    return lax.axis_index("lat"), lax.axis_index("lon")


def shifted(lat, lon, da, do):
    return lax.rem(lat + 4 + da, 4), lax.rem(lon + 64 + do, 64)


def halo_copies(plan, box, land, lat, lon, send_sem, recv_sem):
    return [
        pltpu.make_async_remote_copy(
            src_ref=box.at[pl.ds(start, size)],
            dst_ref=land.at[pl.ds(target, size)],
            send_sem=send_sem.at[k],
            recv_sem=recv_sem.at[k],
            device_id=shifted(lat, lon, *step),
            device_id_type=MESH,
        )
        for k, (start, size, target, step) in enumerate(plan)
    ]


IN_PLAN = ((0, 128, LAT0, (-1, 0)), (128, 48, LON1, (0, -1)), (176, 48, DIAG1, (-1, -1)))
BACK_PLAN = ((LAT0, 128, LAT0, (1, 0)), (LON1, 48, LON1, (0, 1)), (DIAG1, 48, DIAG1, (1, 1)))


def deep_peer(lon, d):
    high, z, y = lon // 32, lax.rem(lon // 4, 8), lax.rem(lon, 4)
    return (high * 8 + lax.rem(z + d, 8)) * 4 + y


def plane_place(lon):
    return (lon // 32) * 4 + lax.rem(lon, 4)


def flat_peer(lon, d):
    z = lax.rem(lon // 4, 8)
    place = lax.rem(plane_place(lon) + d, 8)
    return ((place // 4) * 8 + z) * 4 + lax.rem(place, 4)


def sum_copies(kind, lon, lat, src, dst, send_sem, recv_sem):
    place = plane_place(lon)
    copies = []
    for d in (4, 3, 5, 2, 6, 1, 7) if kind == 1 else (6, 2, 5, 7, 4, 1, 3):
        if kind == 0:
            peer, source, target = flat_peer(lon, d), src.at[lax.rem(place + d, 8)], dst.at[d - 1]
        elif kind == 1:
            peer, source, target = deep_peer(lon, d), src, dst.at[d - 1]
        else:
            peer, source, target = flat_peer(lon, d), src, dst.at[place]
        copies.append(pltpu.make_async_remote_copy(
            src_ref=source, dst_ref=target, send_sem=send_sem.at[kind, d - 1], recv_sem=recv_sem.at[kind, d - 1],
            device_id=(lat, peer), device_id_type=MESH))
    return copies


def add_up(own, slots):
    total = own.astype(F32)
    for d in range(7):
        total = total + slots[d].astype(F32)
    return total


LOCAL = (
    ((4, N, C), BF), ((4, N, C), BF), ((2, ROWS, N), BF), ((N, LAT1), BF), ((N, ROWS - LAT1), BF),
    ((12 * OFFS, 1, N), F32), ((1, C), F32), ((1, C), F32), ((C, 3 * C), BF), ((C, C), BF), ((C, FF), BF), ((C, FF), BF),
    ((LW, N), BF), ((N, LW), BF), ((16, N), BF), ((24, LW), F32), ((2, N, ROWS), BF), ((LAT1, N), BF), ((ROWS - LAT1, N), BF),
)


def block_kernel(*refs):
    count = len(LOCAL)
    far = refs[:count]
    gx_ref, gb_ref = refs[count:count + 2]
    near = refs[count + 2:2 * count + 2]
    (x_ref, ct_ref, pack_ref, place0_ref, place1_ref, tb_ref, g1_ref, g2_ref, wi_ref, wo_ref, wu_ref, wdt_ref,
     join_ref, joint_ref, own_ref, pick_ref, unpack_ref, unplace0_ref, unplace1_ref) = near
    (t24, strips, bias, wit, wq, wk, wv, masked, blocks, probs, dscores, mixed, dbias,
     out_box, land, back_box, back_land, *rest) = refs[2 * count + 2:]
    buffers, rest = (rest[0:6], rest[6:12]), rest[12:]
    near_sem, in_send, in_recv, back_send, back_recv, sum_send, sum_recv = rest
    lat, lon = lat_lon()
    mine = plane_place(lon)

    barrier = pltpu.get_barrier_semaphore()
    for da, do in ((1, 0), (0, 1), (1, 1), (-1, 0), (0, -1), (-1, -1)):
        pl.semaphore_signal(barrier, inc=1, device_id=shifted(lat, lon, da, do), device_id_type=MESH)
    fetches = [pltpu.make_async_copy(far[k], near[k], near_sem.at[k]) for k in range(count)]
    for fetch in fetches:
        fetch.start()
    for d in range(1, 8):
        pl.semaphore_signal(barrier, inc=1, device_id=(lat, deep_peer(lon, d)), device_id_type=MESH)
        pl.semaphore_signal(barrier, inc=1, device_id=(lat, flat_peer(lon, d)), device_id_type=MESH)
    for fetch in fetches[0:3]:
        fetch.wait()

    arrivals = []
    for k, ref in enumerate((x_ref, ct_ref)):
        for a in range(2):
            piece = (nn(pack_ref[0], ref[(2 * a + 1) % 4]) + nn(pack_ref[1], ref[(2 * a + 2) % 4])).astype(BF)
            lanes = slice(a * C, (a + 1) * C)
            land[k, 0:LAT0, lanes] = piece[0:LAT0]
            land[k, OWN1:LON1, lanes] = piece[OWN1:LON1]
            out_box[k, 0:128, lanes] = piece[LAT0:OWN1]
            out_box[k, 128:224, lanes] = piece[LON1:ROWS]
        if k == 0:
            pl.semaphore_wait(barrier, 20)
        arrivals.append(halo_copies(IN_PLAN, out_box.at[k], land.at[k], lat, lon, in_send.at[k], in_recv.at[k]))
        for copy in arrivals[k]:
            copy.start()

    for fetch in fetches[3:]:
        fetch.wait()
    t24[...] = jnp.zeros_like(t24)
    blocks[...] = jnp.zeros_like(blocks)
    for an in range(12):
        t24[an, 0:OFFS, :] = tb_ref[an * OFFS:(an + 1) * OFFS, 0, :]
    prepare_weights(wi_ref, wit, wq, wk, wv)
    expand_bias(lat, joint_ref, own_ref, pick_ref, t24, strips, bias)
    g1, g2 = g1_ref[...], g2_ref[...]

    sums = []
    for g, (red, slots1, part, slots2, whole, full) in enumerate(buffers):
        sums.append([sum_copies(kind, lon, lat, src, dst, sum_send.at[g], sum_recv.at[g])
                     for kind, (src, dst) in enumerate(((red, slots1), (part, slots2), (whole, full)))])

    def sum_first(g):
        fold_bias(g, dbias, join_ref, own_ref, pick_ref, strips, buffers[g][0])
        for copy in sums[g][0]:
            copy.start()

    def sum_second(g):
        red, slots1, part = buffers[g][0:3]
        for copy in sums[g][0]:
            copy.wait_recv()
        part[...] = add_up(red[mine], slots1).astype(BF)
        for copy in sums[g][1]:
            copy.start()

    def sum_third(g):
        part, slots2, whole, full = buffers[g][2:6]
        for copy in sums[g][1]:
            copy.wait_recv()
        total = add_up(part[...], slots2)
        whole[...] = total.astype(BF) if g else fold_one(total, join_ref, own_ref, pick_ref)
        for copy in sums[g][2]:
            copy.start()
        full[mine] = whole[...]

    def sum_last(g):
        for copy in sums[g][2]:
            copy.wait_recv()
        unpack_fold(g, buffers[g][5], gb_ref)

    def windows(k):
        for copy in arrivals[k]:
            copy.wait()
        first = nn(place0_ref[...], land[k, 0:LAT1, :]).astype(BF)
        second = nn(place1_ref[...], land[k, LAT1:ROWS, :]).astype(BF)
        return jnp.concatenate([v[:, a * C:(a + 1) * C] for a in range(2) for v in (first, second)], axis=0)

    state = all_scores(windows(0), lambda: windows(1), g1, g2, wq, wk, wv, wit, wo_ref, wu_ref, wdt_ref, bias,
                       masked, blocks, probs, dscores, mixed, dbias, sum_first)
    gi = all_finish(state, g1, wq, wk, wv, wo_ref, blocks, probs, dscores, lambda: sum_second(0))
    for a in range(2):
        lanes = slice(a * C, (a + 1) * C)
        first = nn(unplace0_ref[...], gi[WINDOWS[2 * a]]).astype(BF)
        second = nn(unplace1_ref[...], gi[WINDOWS[2 * a + 1]]).astype(BF)
        back_land[0:LAT0, lanes] = first[0:LAT0]
        back_land[OWN1:LON1, lanes] = second[OWN1 - LAT1:LON1 - LAT1]
        back_box[LAT0:LAT1, lanes] = first[LAT0:LAT1]
        back_box[LAT1:OWN1, lanes] = second[0:OWN1 - LAT1]
        back_box[LON1:ROWS, lanes] = second[LON1 - LAT1:]
    returns = halo_copies(BACK_PLAN, back_box, back_land, lat, lon, back_send, back_recv)
    for copy in returns:
        copy.start()
    sum_second(1)
    sum_third(0)
    sum_third(1)
    for copy in returns:
        copy.wait()
    for a in range(2):
        for p in range(2):
            gx_ref[(2 * a + 1 + p) % 4] = nn(unpack_ref[p], back_land[:, a * C:(a + 1) * C]).astype(BF)
    sum_last(0)
    for chain in sums:
        for phase in chain[0:2]:
            for copy in phase:
                copy.wait_send()
    sum_last(1)
    for chain in sums:
        for copy in chain[2]:
            copy.wait_send()


def sum_buffers(rows, lanes, whole_rows):
    sent = [pltpu.VMEM(lead + (rows, lanes), BF) for lead in ((8,), (7,), (), (7,))]
    return sent + [pltpu.VMEM(lead + (whole_rows, 128), BF) for lead in ((), (8,))]


def block_call(*operands):
    anywhere = pl.BlockSpec(memory_space=pl.ANY)
    dma = pltpu.SemaphoreType.DMA
    return pl.pallas_call(
        block_kernel,
        out_shape=(pltpu.VMEM((4, N, C), BF), pltpu.VMEM((12 * OFFS, 1, N), F32)),
        in_specs=[anywhere] * len(LOCAL),
        out_specs=(VM, VM),
        scratch_shapes=[pltpu.VMEM(*one) for one in LOCAL] + MAIN_SCRATCH + [
            pltpu.VMEM((2, 224, 2 * C), BF),
            pltpu.VMEM((2, ROWS, 2 * C), BF),
            pltpu.VMEM((ROWS, 2 * C), BF),
            pltpu.VMEM((ROWS, 2 * C), BF),
        ] + sum_buffers(16, LW, 32) + sum_buffers(16, 128, 16) + [
            dma((len(LOCAL),)), dma((2, 3)), dma((2, 3)), dma((3,)), dma((3,)), dma((2, 3, 7)), dma((2, 3, 7)),
        ],
        compiler_params=pltpu.CompilerParams(collective_id=0, has_side_effects=True, vmem_limit_bytes=60 * 1024 * 1024),
    )(*operands)


def on_device(block_input, cotangent, first_gain, second_gain, input_weight, output_weight, up_weight,
              down_weight, bias_table):
    join, own, pick = fold_consts()
    pack, place0, place1 = piece_consts()
    as_bf = lambda v: jnp.asarray(v, BF)
    gx, gb = block_call(
        block_input.reshape(4, N, C), cotangent.reshape(4, N, C), as_bf(pack), as_bf(place0), as_bf(place1),
        bias_table.reshape(12 * OFFS, 1, N),
        first_gain[None], second_gain[None], input_weight, output_weight, up_weight, down_weight.T,
        as_bf(join), as_bf(join.T), as_bf(own), jnp.asarray(pick), as_bf(pack.transpose(0, 2, 1)), as_bf(place0.T), as_bf(place1.T))
    return gx.reshape(block_input.shape), gb.reshape(bias_table.shape)


def solution(mesh):
    P = jax.sharding.PartitionSpec
    in_specs = (
        P(None, "lat", "lon", None),
        P(None, "lat", "lon", None),
        P(), P(), P(), P(), P(), P(),
        P(None, "lat", None, None, None),
    )
    out_specs = (P(None, "lat", "lon", None), P(None, "lat", None, None, None))
    return jax.shard_map(on_device, mesh=mesh, in_specs=in_specs, out_specs=out_specs, check_vma=False)
```

```python
import functools
import numpy as np
import jax
import jax.numpy as jnp
from jax import lax
from jax.experimental import pallas as pl
from jax.experimental.pallas import tpu as pltpu

BF = jnp.bfloat16
F32 = jnp.float32
HEADS, WZ, WH, WW = 6, 2, 6, 12
HD = 32
C = 192
FF = 768
N = 144
PS = WZ * WH
OFFS = 2 * WW - 1
LW = 384
EPS = 1e-05
SCALE = HD ** -0.5
NEG = -1e30
LOG2E = 1.4426950408889634


def nn(a, b):
    return lax.dot_general(a, b, (((1,), (0,)), ((), ())), preferred_element_type=F32)


def nt(a, b):
    return lax.dot_general(a, b, (((1,), (1,)), ((), ())), preferred_element_type=F32)


def tn(a, b):
    return lax.dot_general(a, b, (((0,), (0,)), ((), ())), preferred_element_type=F32)


def fold_consts():
    join = np.zeros((LW, N), np.float32)
    own = np.zeros((16, N), np.float32)
    for p in range(WZ):
        for q in range(WZ):
            for s in range(WH):
                for t in range(WH):
                    m = ((p * WZ + q) * WH + s) * WH + t
                    own[q * WH + t, m] = 1
                    join[p * WH + s:OFFS * PS:PS, m] = 1
    pick = np.zeros((24, LW), np.float32)
    for r in range(OFFS):
        pick[r, r * PS:(r + 1) * PS] = 1
    return join, own, pick


def normalize(v):
    centred = v - jnp.mean(v, axis=-1, keepdims=True)
    rs = lax.rsqrt(jnp.mean(centred * centred, axis=-1, keepdims=True) + EPS)
    return centred * rs, rs


def norm_back(g, xh, rs):
    return rs * (g - jnp.mean(g, axis=-1, keepdims=True) - xh * jnp.mean(g * xh, axis=-1, keepdims=True))


def gelu_slope(h):
    cdf = 0.5 + 0.5 * lax.erf(h * 0.7071067811865476)
    return cdf + h * (jnp.exp(-0.5 * (h * h)) * 0.3989422804014327)


def expand_bias(lat, joint_ref, own_ref, pick_ref, t24, strips, bias):
    table = t24[...].reshape(12 * 24, N)
    hi = table.astype(BF)
    low = (table - hi.astype(F32)).astype(BF)
    pick = pick_ref[...][None] * LOG2E
    for qt in range(PS):
        own = own_ref[qt:qt + 1, :]
        wide = nn(hi * own, joint_ref[...]) + nn(low * own, joint_ref[...])
        strips[:, qt, :] = jnp.sum(wide.reshape(12, 24, LW) * pick, axis=1)
    row = lax.broadcasted_iota(jnp.int32, (N, N), 0).astype(F32)
    col = lax.broadcasted_iota(jnp.int32, (N, N), 1).astype(F32)

    def place(v):
        ps = v - PS * jnp.floor((v + 0.5) * (1.0 / PS))
        upper = (ps >= WH).astype(F32)
        s = ps - WH * upper
        return upper, (s >= WH // 2).astype(F32)

    rp, rs = place(row)
    cp, cs = place(col)
    last_band = (lat == 3).astype(F32)
    apart_rows = jnp.abs(rs - cs) * last_band
    apart_levels = jnp.abs(rp - cp)
    for a in range(2):
        apart = apart_rows + apart_levels if a else apart_rows
        excluded = jnp.where(apart > 0.5, NEG, 0.0)
        for an in range(a * HEADS, (a + 1) * HEADS):
            strip = strips[an, 0:PS, :]
            for j in range(WW):
                lo = (WW - 1 - j) * PS
                rows = slice(j * PS, (j + 1) * PS)
                bias[an, rows, :] = strip[:, lo:lo + N] + excluded[rows]


GROUPS = ((0, 4), (4, 6))


def head_picks():
    lane = lax.broadcasted_iota(jnp.int32, (1, 128), 1)
    return [((lane >= n * HD % 128) & (lane < n * HD % 128 + HD)).astype(F32) for n in range(HEADS)]


WINDOWS = [slice(w * N, (w + 1) * N) for w in range(4)]


def all_scores(x, late_ct, g1, g2, wq, wk, wv, wqkvt, wo_ref, wu_ref, wdt_ref,
               bias, masked, blocks, probs, dscores, mixed, dbias, after_group):
    picks16 = [v.astype(BF) for v in head_picks()]

    def by_head(w, v, kind):
        for n in range(HEADS):
            if n < 4:
                masked[kind, w, n * N:(n + 1) * N, :] = v[:, 0:128] * picks16[n]
            else:
                masked[kind, w, n * N:(n + 1) * N, 0:64] = v[:, 128:C] * picks16[n][:, 0:64]

    x = x.astype(F32)
    xh1, rs1 = normalize(x)
    xn1 = (xh1 * g1).astype(BF)
    keys = nn(xn1, wk[...]).astype(BF)
    values = nn(xn1, wv[...]).astype(BF)
    qkvt = [nt(wqkvt[...], xn1[rows]).astype(BF) for rows in WINDOWS]
    for w, rows in enumerate(WINDOWS):
        by_head(w, keys[rows], 0)
        by_head(w, values[rows], 1)
        for n in range(HEADS):
            for k in range(2):
                blocks[k, w, n * HD:(n + 1) * HD, n * N:(n + 1) * N] = (
                    qkvt[w][(2 - k) * C + n * HD:(2 - k) * C + (n + 1) * HD])
    for first, end in GROUPS:
        width = min(C, end * HD) - first * HD
        for w in range(4):
            s_all = nn(masked[0, w, first * N:end * N, 0:width], qkvt[w][first * HD:end * HD, :])
            for n in range(first, end):
                s = s_all[(n - first) * N:(n - first + 1) * N] * (SCALE * LOG2E) + bias[(w // 2) * HEADS + n]
                e = jnp.exp2(s - jnp.max(s, axis=0, keepdims=True))
                p = (e * (1.0 / jnp.sum(e, axis=0, keepdims=True))).astype(BF)
                probs[w, n * N:(n + 1) * N, :] = p
    for w in range(4):
        mixed[w] = nn(blocks[0, w], probs[w]).astype(BF)
    ct = late_ct()
    attn = jnp.concatenate([tn(mixed[w], wo_ref[...]) for w in range(4)], axis=0).astype(BF)
    y = x + attn.astype(F32)
    xh2, rs2 = normalize(y)
    xn2 = (xh2 * g2).astype(BF)
    dxn2 = jnp.zeros((4 * N, C), F32)
    for f in range(FF // 256):
        up = wu_ref[:, f * 256:(f + 1) * 256]
        h = nn(xn2, up)
        da = nn(ct, wdt_ref[:, f * 256:(f + 1) * 256])
        dh = (da * gelu_slope(h)).astype(BF)
        dxn2 = dxn2 + nt(dh, up)
    dy = ct.astype(F32) + norm_back(dxn2 * g2, xh2, rs2)
    gattn = dy.astype(BF)
    dmixt = [nt(wo_ref[...], gattn[rows]).astype(BF) for rows in WINDOWS]
    for group, (first, end) in enumerate(GROUPS):
        width = min(C, end * HD) - first * HD
        span = slice(first * HD, first * HD + width)
        parts = [[], [], [], []]
        for w in range(4):
            dp_all = nn(masked[1, w, first * N:end * N, 0:width], dmixt[w][span, :])
            for n in range(first, end):
                dp = dp_all[(n - first) * N:(n - first + 1) * N]
                p = probs[w, n * N:(n + 1) * N, :].astype(F32)
                pd = p * dp
                ds = pd - p * jnp.sum(pd, axis=0, keepdims=True)
                parts[w].append(ds)
                dscores[w, n * N:(n + 1) * N, :] = ds.astype(BF)
            if w % 2:
                for n in range(first, end):
                    dbias[(w // 2) * HEADS + n] = parts[w - 1][n - first] + parts[w][n - first]
        after_group(group)
    return xh1, rs1, xn1, dy, gattn


def all_finish(state, g1, wq, wk, wv, wo_ref, blocks, probs, dscores, halfway):
    picks = head_picks()
    xh1, rs1, xn1, dy, gattn = state
    queries = nn(xn1, wq[...]).astype(BF)
    dmix = nt(gattn, wo_ref[...]).astype(BF)
    dqs = [nn(blocks[1, w], dscores[w]) for w in range(4)]
    dks, dvs = [[], [], [], []], [[], [], [], []]
    for first, end in GROUPS:
        width = min(C, end * HD) - first * HD
        span = slice(first * HD, first * HD + width)
        for w, rows in enumerate(WINDOWS):
            dk_all = nn(dscores[w, first * N:end * N, :], queries[rows, span])
            dv_all = nn(probs[w, first * N:end * N, :], dmix[rows, span])
            for store, full in ((dks, dk_all), (dvs, dv_all)):
                total = jnp.zeros((N, width), F32)
                for n in range(first, end):
                    total = total + full[(n - first) * N:(n - first + 1) * N] * picks[n][:, 0:width]
                store[w].append(total)
    halfway()
    dq = jnp.concatenate([(dqs[w] * SCALE).astype(BF).T for w in range(4)], axis=0)
    dk = (jnp.concatenate([jnp.concatenate(dks[w], axis=1) for w in range(4)], axis=0) * SCALE).astype(BF)
    dv = jnp.concatenate([jnp.concatenate(dvs[w], axis=1) for w in range(4)], axis=0).astype(BF)
    dxn1 = nt(dq, wq[...]) + nt(dk, wk[...]) + nt(dv, wv[...])
    return (dy + norm_back(dxn1.astype(BF).astype(F32) * g1, xh1, rs1)).astype(BF)


def group_tables(group):
    first, end = GROUPS[group]
    return [a * HEADS + n for a in range(2) for n in range(first, end)]


def diagonals(an, dbias):
    total = jnp.zeros((PS, LW), F32)
    for j in range(WW):
        lo = (WW - 1 - j) * PS
        total = total + jnp.pad(dbias[an, j * PS:(j + 1) * PS, :], ((0, 0), (lo, LW - N - lo)))
    return total


def to_columns(count, rows_of, join_ref, own_ref, pick_ref):
    total = jnp.zeros((count * 24, N), F32)
    for qt in range(PS):
        rows = (rows_of(qt)[:, None, :] * pick_ref[...][None]).reshape(count * 24, LW).astype(BF)
        total = total + nn(rows, join_ref[...]) * own_ref[qt:qt + 1, :].astype(F32)
    return total


def fold_bias(group, dbias, join_ref, own_ref, pick_ref, strips, red):
    tables = group_tables(group)
    count = len(tables)
    if group == 0:
        for k, an in enumerate(tables):
            red[k] = jnp.concatenate([diagonals(an, dbias), jnp.zeros((16 - PS, LW), F32)], axis=0).astype(BF)
        return
    for k, an in enumerate(tables):
        strips[k, 0:PS, :] = diagonals(an, dbias)
    total = to_columns(count, lambda qt: strips[0:count, qt, :], join_ref, own_ref, pick_ref)
    tails = jnp.zeros((24, 128), F32)
    for k in range(count):
        tail = jnp.concatenate([total[k * 24:(k + 1) * 24, 128:N], jnp.zeros((24, 112), F32)], axis=1)
        tails = tails + (pltpu.roll(tail, 16 * k, 1) if k else tail)
    rows = red.shape[0] * red.shape[1]
    red[...] = jnp.concatenate(
        [total[:, 0:128], tails, jnp.zeros((rows - (count + 1) * 24, 128), F32)], axis=0).astype(BF).reshape(red.shape)


def fold_one(strip, join_ref, own_ref, pick_ref):
    total = to_columns(1, lambda qt: strip[qt:qt + 1], join_ref, own_ref, pick_ref)
    tails = jnp.zeros((8, 128), F32)
    for g in range(3):
        tail = jnp.concatenate([total[8 * g:8 * g + 8, 128:N], jnp.zeros((8, 112), F32)], axis=1)
        tails = tails + (pltpu.roll(tail, 16 * g, 1) if g else tail)
    return jnp.concatenate([total[:, 0:128], tails], axis=0).astype(BF)


def unpack_fold(group, full, gb_ref):
    tables = group_tables(group)
    count = len(tables)
    if group == 0:
        for k, an in enumerate(tables):
            rows = full[k].astype(F32)
            gb_ref[an * OFFS:(an + 1) * OFFS, 0, 0:128] = rows[0:OFFS]
            for g in range(3):
                size = min(8, OFFS - 8 * g)
                place = slice(an * OFFS + 8 * g, an * OFFS + 8 * g + size)
                gb_ref[place, 0, 128:N] = rows[24:24 + size, 16 * g:16 * (g + 1)]
        return
    rows = full[...].astype(F32).reshape(full.shape[0] * full.shape[1], 128)
    for k, an in enumerate(tables):
        place = slice(an * OFFS, (an + 1) * OFFS)
        gb_ref[place, 0, 0:128] = rows[k * 24:k * 24 + OFFS]
        gb_ref[place, 0, 128:N] = rows[count * 24:count * 24 + OFFS, 16 * k:16 * (k + 1)]


def prepare_weights(wi_ref, wit, wq, wk, wv):
    wit[...] = wi_ref[...].T
    for k, ref in enumerate((wq, wk, wv)):
        ref[...] = wi_ref[:, k * C:(k + 1) * C]


VM = pl.BlockSpec(memory_space=pltpu.VMEM)

MAIN_SCRATCH = [
    pltpu.VMEM((12, 24, N), F32),
    pltpu.VMEM((12, 16, LW), F32),
    pltpu.VMEM((12, N, N), F32),
    pltpu.VMEM((3 * C, C), BF),
    pltpu.VMEM((C, C), BF),
    pltpu.VMEM((C, C), BF),
    pltpu.VMEM((C, C), BF),
    pltpu.VMEM((2, 4, HEADS * N, 128), BF),
    pltpu.VMEM((2, 4, C, HEADS * N), BF),
    pltpu.VMEM((4, HEADS * N, N), BF),
    pltpu.VMEM((4, HEADS * N, N), BF),
    pltpu.VMEM((4, C, N), BF),
    pltpu.VMEM((12, N, N), F32),
]


PIECE0, PIECE1 = 80, 48
LAT0, LAT1, OWN1, LON1, DIAG1, ROWS = 80, 160, 208, 256, 304, 352
MESH = pl.DeviceIdType.MESH


def piece_consts():
    pack = np.zeros((2, ROWS, N), np.float32)
    place0 = np.zeros((N, LAT1), np.float32)
    place1 = np.zeros((N, ROWS - LAT1), np.float32)
    for p in range(2):
        for h in range(6):
            own = h >= 3
            s = h - 3 if own else h + 3
            for w in range(24):
                e = (w - 6) % 24
                if e < 12:
                    row = (0 if own else LAT0) + (e * 2 + p) * 3 + s % 3
                    place0[e * PS + p * WH + s, row] = 1
                else:
                    e -= 12
                    base = (OWN1 if own else LAT1) if e < 6 else (LON1 if own else DIAG1)
                    row = base + ((e % 6) * 2 + p) * 3 + s % 3
                    place1[e * PS + p * WH + s, row - LAT1] = 1
                pack[p, row, h * 24 + w] = 1
    return pack, place0, place1


def lat_lon():
    return lax.axis_index("lat"), lax.axis_index("lon")


def shifted(lat, lon, da, do):
    return lax.rem(lat + 4 + da, 4), lax.rem(lon + 64 + do, 64)


def halo_copies(plan, box, land, lat, lon, send_sem, recv_sem):
    return [
        pltpu.make_async_remote_copy(
            src_ref=box.at[pl.ds(start, size)],
            dst_ref=land.at[pl.ds(target, size)],
            send_sem=send_sem.at[k],
            recv_sem=recv_sem.at[k],
            device_id=shifted(lat, lon, *step),
            device_id_type=MESH,
        )
        for k, (start, size, target, step) in enumerate(plan)
    ]


IN_PLAN = ((176, 48, DIAG1, (-1, -1)), (128, 48, LON1, (0, -1)), (0, 128, LAT0, (-1, 0)))
BACK_PLAN = ((DIAG1, 48, DIAG1, (1, 1)), (LON1, 48, LON1, (0, 1)), (LAT0, 128, LAT0, (1, 0)))


def deep_peer(lon, d):
    high, z, y = lon // 32, lax.rem(lon // 4, 8), lax.rem(lon, 4)
    return (high * 8 + lax.rem(z + d, 8)) * 4 + y


def plane_place(lon):
    return (lon // 32) * 4 + lax.rem(lon, 4)


def flat_peer(lon, d):
    z = lax.rem(lon // 4, 8)
    place = lax.rem(plane_place(lon) + d, 8)
    return ((place // 4) * 8 + z) * 4 + lax.rem(place, 4)


def sum_copies(kind, lon, lat, src, dst, send_sem, recv_sem):
    place = plane_place(lon)
    copies = []
    for d in (4, 3, 5, 2, 6, 1, 7) if kind == 1 else (6, 2, 5, 7, 4, 1, 3):
        if kind == 0:
            peer, source, target = flat_peer(lon, d), src.at[lax.rem(place + d, 8)], dst.at[d - 1]
        elif kind == 1:
            peer, source, target = deep_peer(lon, d), src, dst.at[d - 1]
        else:
            peer, source, target = flat_peer(lon, d), src, dst.at[place]
        copies.append(pltpu.make_async_remote_copy(
            src_ref=source, dst_ref=target, send_sem=send_sem.at[kind, d - 1], recv_sem=recv_sem.at[kind, d - 1],
            device_id=(lat, peer), device_id_type=MESH))
    return copies


def add_up(own, slots):
    total = own.astype(F32)
    for d in range(7):
        total = total + slots[d].astype(F32)
    return total


LOCAL = (
    ((4, N, C), BF), ((4, N, C), BF), ((2, ROWS, N), BF), ((N, LAT1), BF), ((N, ROWS - LAT1), BF),
    ((12 * OFFS, 1, N), F32), ((1, C), F32), ((1, C), F32), ((C, 3 * C), BF), ((C, C), BF), ((C, FF), BF), ((C, FF), BF),
    ((LW, N), BF), ((N, LW), BF), ((16, N), BF), ((24, LW), F32), ((2, N, ROWS), BF), ((LAT1, N), BF), ((ROWS - LAT1, N), BF),
)


def block_kernel(*refs):
    count = len(LOCAL)
    far = refs[:count]
    gx_ref, gb_ref = refs[count:count + 2]
    near = refs[count + 2:2 * count + 2]
    (x_ref, ct_ref, pack_ref, place0_ref, place1_ref, tb_ref, g1_ref, g2_ref, wi_ref, wo_ref, wu_ref, wdt_ref,
     join_ref, joint_ref, own_ref, pick_ref, unpack_ref, unplace0_ref, unplace1_ref) = near
    (t24, strips, bias, wit, wq, wk, wv, masked, blocks, probs, dscores, mixed, dbias,
     out_box, land, back_box, back_land, *rest) = refs[2 * count + 2:]
    buffers, rest = (rest[0:6], rest[6:12]), rest[12:]
    near_sem, in_send, in_recv, back_send, back_recv, sum_send, sum_recv = rest
    lat, lon = lat_lon()
    mine = plane_place(lon)

    barrier = pltpu.get_barrier_semaphore()
    for da, do in ((1, 0), (0, 1), (1, 1), (-1, 0), (0, -1), (-1, -1)):
        pl.semaphore_signal(barrier, inc=1, device_id=shifted(lat, lon, da, do), device_id_type=MESH)
    fetches = [pltpu.make_async_copy(far[k], near[k], near_sem.at[k]) for k in range(count)]
    for fetch in fetches:
        fetch.start()
    for d in range(1, 8):
        pl.semaphore_signal(barrier, inc=1, device_id=(lat, deep_peer(lon, d)), device_id_type=MESH)
        pl.semaphore_signal(barrier, inc=1, device_id=(lat, flat_peer(lon, d)), device_id_type=MESH)
    for fetch in fetches[0:3]:
        fetch.wait()

    arrivals = []
    for k, ref in enumerate((x_ref, ct_ref)):
        for a in range(2):
            piece = (nn(pack_ref[0], ref[(2 * a + 1) % 4]) + nn(pack_ref[1], ref[(2 * a + 2) % 4])).astype(BF)
            lanes = slice(a * C, (a + 1) * C)
            land[k, 0:LAT0, lanes] = piece[0:LAT0]
            land[k, OWN1:LON1, lanes] = piece[OWN1:LON1]
            out_box[k, 0:128, lanes] = piece[LAT0:OWN1]
            out_box[k, 128:224, lanes] = piece[LON1:ROWS]
        if k == 0:
            pl.semaphore_wait(barrier, 20)
        arrivals.append(halo_copies(IN_PLAN, out_box.at[k], land.at[k], lat, lon, in_send.at[k], in_recv.at[k]))
        for copy in arrivals[k]:
            copy.start()

    for fetch in fetches[3:]:
        fetch.wait()
    t24[...] = jnp.zeros_like(t24)
    blocks[...] = jnp.zeros_like(blocks)
    for an in range(12):
        t24[an, 0:OFFS, :] = tb_ref[an * OFFS:(an + 1) * OFFS, 0, :]
    prepare_weights(wi_ref, wit, wq, wk, wv)
    expand_bias(lat, joint_ref, own_ref, pick_ref, t24, strips, bias)
    g1, g2 = g1_ref[...], g2_ref[...]

    sums = []
    for g, (red, slots1, part, slots2, whole, full) in enumerate(buffers):
        sums.append([sum_copies(kind, lon, lat, src, dst, sum_send.at[g], sum_recv.at[g])
                     for kind, (src, dst) in enumerate(((red, slots1), (part, slots2), (whole, full)))])

    def sum_first(g):
        fold_bias(g, dbias, join_ref, own_ref, pick_ref, strips, buffers[g][0])
        for copy in sums[g][0]:
            copy.start()

    def sum_second(g):
        red, slots1, part = buffers[g][0:3]
        for copy in sums[g][0]:
            copy.wait_recv()
        part[...] = add_up(red[mine], slots1).astype(BF)
        for copy in sums[g][1]:
            copy.start()

    def sum_third(g):
        part, slots2, whole, full = buffers[g][2:6]
        for copy in sums[g][1]:
            copy.wait_recv()
        total = add_up(part[...], slots2)
        whole[...] = total.astype(BF) if g else fold_one(total, join_ref, own_ref, pick_ref)
        for copy in sums[g][2]:
            copy.start()
        full[mine] = whole[...]

    def sum_last(g):
        for copy in sums[g][2]:
            copy.wait_recv()
        unpack_fold(g, buffers[g][5], gb_ref)

    def windows(k):
        for copy in arrivals[k]:
            copy.wait_recv()
        first = nn(place0_ref[...], land[k, 0:LAT1, :]).astype(BF)
        second = nn(place1_ref[...], land[k, LAT1:ROWS, :]).astype(BF)
        return jnp.concatenate([v[:, a * C:(a + 1) * C] for a in range(2) for v in (first, second)], axis=0)

    state = all_scores(windows(0), lambda: windows(1), g1, g2, wq, wk, wv, wit, wo_ref, wu_ref, wdt_ref, bias,
                       masked, blocks, probs, dscores, mixed, dbias, sum_first)
    gi = all_finish(state, g1, wq, wk, wv, wo_ref, blocks, probs, dscores, lambda: sum_second(0))
    for a in range(2):
        lanes = slice(a * C, (a + 1) * C)
        first = nn(unplace0_ref[...], gi[WINDOWS[2 * a]]).astype(BF)
        second = nn(unplace1_ref[...], gi[WINDOWS[2 * a + 1]]).astype(BF)
        back_land[0:LAT0, lanes] = first[0:LAT0]
        back_land[OWN1:LON1, lanes] = second[OWN1 - LAT1:LON1 - LAT1]
        back_box[LAT0:LAT1, lanes] = first[LAT0:LAT1]
        back_box[LAT1:OWN1, lanes] = second[0:OWN1 - LAT1]
        back_box[LON1:ROWS, lanes] = second[LON1 - LAT1:]
    returns = halo_copies(BACK_PLAN, back_box, back_land, lat, lon, back_send, back_recv)
    for copy in returns:
        copy.start()
    sum_second(1)
    sum_third(0)
    sum_third(1)
    for copy in returns:
        copy.wait_recv()
    for a in range(2):
        for p in range(2):
            gx_ref[(2 * a + 1 + p) % 4] = nn(unpack_ref[p], back_land[:, a * C:(a + 1) * C]).astype(BF)
    sum_last(0)
    for copy in arrivals[0] + arrivals[1] + returns:
        copy.wait_send()
    for chain in sums:
        for phase in chain[0:2]:
            for copy in phase:
                copy.wait_send()
    sum_last(1)
    for chain in sums:
        for copy in chain[2]:
            copy.wait_send()


def sum_buffers(rows, lanes, whole_rows):
    sent = [pltpu.VMEM(lead + (rows, lanes), BF) for lead in ((8,), (7,), (), (7,))]
    return sent + [pltpu.VMEM(lead + (whole_rows, 128), BF) for lead in ((), (8,))]


def block_call(*operands):
    anywhere = pl.BlockSpec(memory_space=pl.ANY)
    dma = pltpu.SemaphoreType.DMA
    return pl.pallas_call(
        block_kernel,
        out_shape=(pltpu.VMEM((4, N, C), BF), pltpu.VMEM((12 * OFFS, 1, N), F32)),
        in_specs=[anywhere] * len(LOCAL),
        out_specs=(VM, VM),
        scratch_shapes=[pltpu.VMEM(*one) for one in LOCAL] + MAIN_SCRATCH + [
            pltpu.VMEM((2, 224, 2 * C), BF),
            pltpu.VMEM((2, ROWS, 2 * C), BF),
            pltpu.VMEM((ROWS, 2 * C), BF),
            pltpu.VMEM((ROWS, 2 * C), BF),
        ] + sum_buffers(16, LW, 32) + sum_buffers(16, 128, 16) + [
            dma((len(LOCAL),)), dma((2, 3)), dma((2, 3)), dma((3,)), dma((3,)), dma((2, 3, 7)), dma((2, 3, 7)),
        ],
        compiler_params=pltpu.CompilerParams(collective_id=0, has_side_effects=True, vmem_limit_bytes=60 * 1024 * 1024),
    )(*operands)


def on_device(block_input, cotangent, first_gain, second_gain, input_weight, output_weight, up_weight,
              down_weight, bias_table):
    join, own, pick = fold_consts()
    pack, place0, place1 = piece_consts()
    as_bf = lambda v: jnp.asarray(v, BF)
    gx, gb = block_call(
        block_input.reshape(4, N, C), cotangent.reshape(4, N, C), as_bf(pack), as_bf(place0), as_bf(place1),
        bias_table.reshape(12 * OFFS, 1, N),
        first_gain[None], second_gain[None], input_weight, output_weight, up_weight, down_weight.T,
        as_bf(join), as_bf(join.T), as_bf(own), jnp.asarray(pick), as_bf(pack.transpose(0, 2, 1)), as_bf(place0.T), as_bf(place1.T))
    return gx.reshape(block_input.shape), gb.reshape(bias_table.shape)


def solution(mesh):
    P = jax.sharding.PartitionSpec
    in_specs = (
        P(None, "lat", "lon", None),
        P(None, "lat", "lon", None),
        P(), P(), P(), P(), P(), P(),
        P(None, "lat", None, None, None),
    )
    out_specs = (P(None, "lat", "lon", None), P(None, "lat", None, None, None))
    return jax.shard_map(on_device, mesh=mesh, in_specs=in_specs, out_specs=out_specs, check_vma=False)
```
